256 devices in a mesh: tile: 32 (over x_lo, z, core), sub: 8 (over x_hi, y).
Axes of the slice: x: 4 (x_hi: 2, x_lo: 2; x = x_hi * 2 + x_lo), y: 4, z: 8, core: 2. Of those that a mesh axis runs over, the one named last changes fastest.
Arguments:
- initial_heat: float32 [2, 256, 256, 256], P(None, 'tile', 'sub'), may hold values from -8 to 8
- cond_level: int32 [2, 256, 256, 256], P(None, 'tile', 'sub'), may hold values from 0 to 15
- cond_table: float32 [16], replicated, may hold values from 0.1 to 1
- lift_weight: float32 [2, 32], replicated, may hold values from -4 to 4
- lift_bias: float32 [32], replicated, may hold values from -3 to 3
- mix_weight: float32 [32, 32], replicated, may hold values from -1 to 1
- mix_bias: float32 [32], replicated, may hold values from -3 to 3
- proj_weight: float32 [32], replicated, may hold values from -1 to 1
- spectral_weight: float32 [8, 32, 16, 2, 32, 32], P('sub', 'tile'), may hold values from -1 to 1
- target_field: float32 [2, 128, 128, 128], P(None, 'tile', 'sub'), may hold values from -8 to 8
Outputs:
- prediction: float32 [2, 128, 128, 128], P(None, 'tile', 'sub')
- spectral_grad: float32 [8, 32, 16, 2, 32, 32], P('sub', 'tile')
The draws below stay inside these ranges and needn't reach their ends.
All inputs are finite; a program needn't handle non-finite values.
Results may differ from the reference program's by a relative error of at most 0.00012.
Values sent between devices are 32-bit elements; how exact they have to be, the bound alone decides.
No kernel may reach another device: no remote copies, remote signals or barrier semaphores. Data moves between devices by JAX's collectives and lax.ppermute only.
A program may use at most 128 MiB of HBM per device.

```python
import math
import jax
import jax.numpy as jnp
from jax import lax

NC = 128
C = 32
M = 16
B = 2
STEPS = 4
RF = 2
LEVELS = 16
FN = 256
PAIRS = 32
KZB = 8


def wave_profile(source_key, samples, length, mode_count):
    amplitude_key, phase_key = jax.random.split(source_key)
    amplitudes = jax.random.uniform(amplitude_key, (samples, mode_count), jnp.float32, -1.0, 1.0) / math.sqrt(mode_count)
    phases = jax.random.uniform(phase_key, (samples, mode_count), jnp.float32, 0.0, 2.0 * math.pi)
    cycles = jnp.arange(length, dtype=jnp.int32)[:, None] * jnp.arange(mode_count, dtype=jnp.int32)[None, :] % length
    angles = cycles.astype(jnp.float32) * (2.0 * math.pi / length)
    return jnp.sum(amplitudes[:, None, :] * jnp.cos(angles[None, :, :] + phases[:, None, :]), axis=2)


def smooth_field(source_key, samples, length, scale):
    accumulated = jnp.zeros((samples, length, length, length), jnp.float32)
    for term_index in range(4):
        subkeys = jax.random.split(jax.random.fold_in(source_key, term_index), 3)
        along_x = wave_profile(subkeys[0], samples, length, 8)
        along_y = wave_profile(subkeys[1], samples, length, 8)
        along_z = wave_profile(subkeys[2], samples, length, 16)
        accumulated = accumulated + along_x[:, :, None, None] * along_y[:, None, :, None] * along_z[:, None, None, :]
    return scale * accumulated


def draw_initial_heat(key, part):
    key = jax.random.fold_in(key, 11)
    rough_key, smooth_key = jax.random.split(key)
    grid_shape = (B, FN, FN, FN)
    rough_part = jax.random.normal(rough_key, grid_shape, jnp.float32)
    smooth_part = smooth_field(smooth_key, B, FN, 2.0)
    return jnp.clip(rough_part + smooth_part, -8.0, 8.0)


def draw_target_field(key, part):
    key = jax.random.fold_in(key, 23)
    rough_key, smooth_key = jax.random.split(key)
    grid_shape = (B, NC, NC, NC)
    rough_part = 0.5 * jax.random.normal(rough_key, grid_shape, jnp.float32)
    smooth_part = smooth_field(smooth_key, B, NC, 1.5)
    return jnp.clip(rough_part + smooth_part, -8.0, 8.0)


def place_ends(values, stream_key, least, high):
    longest = values.shape.index(max(values.shape))
    spots = []
    for shift in (0, 1):
        where = [jax.random.randint(jax.random.fold_in(stream_key, axis), (), 0, length) for axis, length in enumerate(values.shape)]
        where[longest] = (where[longest] + shift) % values.shape[longest]
        spots.append(tuple(where))
    return values.at[spots[0]].set(least).at[spots[1]].set(high)


def shard_levels(stream_key, extent, cuts, smallest, high):
    gain = 1.0
    for position, parts in cuts:
        draws = jax.random.uniform(jax.random.fold_in(jax.random.fold_in(stream_key, 6), position), (parts,), jnp.float32, smallest / len(cuts), high / len(cuts))
        gain = gain * jnp.repeat(jnp.exp(draws), extent[position] // parts).reshape((-1,) + (1,) * (len(extent) - 1 - position))
    return gain


def scatter_about(stream_key, extent, spread, limit, shards=(), held_as=jnp.bfloat16):
    drawn = spread * jax.random.normal(stream_key, extent, jnp.float32)
    if shards:
        drawn = drawn * shard_levels(stream_key, extent, shards, -0.22, 0.18)
    return jnp.clip(drawn, -limit, limit).astype(held_as)


def setup_inputs(seed: int = 0) -> dict:
    streams_of = jax.random.split(jax.random.key(seed), 11)
    return {
        "initial_heat": draw_initial_heat(jax.random.fold_in(streams_of[10], 71), 0),
        "cond_level": place_ends(jax.random.randint(streams_of[1], (B, FN, FN, FN), 0, LEVELS), jax.random.fold_in(streams_of[1], 1), 0, LEVELS - 1).astype(jnp.int32),
        "cond_table": jnp.clip(jnp.exp(jax.random.uniform(streams_of[2], (LEVELS,), jnp.float32, math.log(0.1), math.log(1.0))), 0.1, 1.0),
        "lift_weight": scatter_about(streams_of[3], (2, C), 1.0, 4.0, (), jnp.float32),
        "lift_bias": scatter_about(streams_of[4], (C,), 0.5, 3.0, (), jnp.float32),
        "mix_weight": scatter_about(streams_of[5], (C, C), C ** -0.5, 1.0, (), jnp.float32),
        "mix_bias": scatter_about(streams_of[6], (C,), 0.5, 3.0, (), jnp.float32),
        "proj_weight": scatter_about(streams_of[7], (C,), C ** -0.5, 1.0, (), jnp.float32),
        "spectral_weight": scatter_about(streams_of[8], (KZB, PAIRS, M, 2, C, C), C ** -0.5, 1.0, ((0, 8), (1, 32)), jnp.float32),
        "target_field": draw_target_field(jax.random.fold_in(streams_of[10], 71), 0),
    }


time_step = 0.16
highest = lax.Precision.HIGHEST

def dft_tables(length, mode_count, centered):
    frequency = jnp.arange(mode_count, dtype=jnp.int32)
    if centered:
        frequency = jnp.where(frequency >= mode_count // 2, frequency - mode_count, frequency)
    cycles = jnp.arange(length, dtype=jnp.int32)[:, None] * frequency[None, :] % length
    angles = cycles.astype(jnp.float32) * (2.0 * math.pi / length)
    return (jnp.cos(angles), jnp.sin(angles))

def heat_step(field, cond):
    field_pad = jnp.pad(field, ((0, 0), (0, 0), (0, 0), (1, 1)))
    cond_pad = jnp.pad(cond, ((0, 0), (0, 0), (0, 0), (1, 1)))
    rows_x = field.shape[1] - 2
    rows_y = field.shape[2] - 2
    rows_z = field.shape[3]
    center = field_pad[:, 1:-1, 1:-1, 1:-1]
    center_cond = cond_pad[:, 1:-1, 1:-1, 1:-1]
    change = jnp.zeros_like(center)
    for shift_x, shift_y, shift_z in ((2, 1, 1), (0, 1, 1), (1, 2, 1), (1, 0, 1), (1, 1, 2), (1, 1, 0)):
        near = field_pad[:, shift_x:shift_x + rows_x, shift_y:shift_y + rows_y, shift_z:shift_z + rows_z]
        near_cond = cond_pad[:, shift_x:shift_x + rows_x, shift_y:shift_y + rows_y, shift_z:shift_z + rows_z]
        change = change + 0.5 * (center_cond + near_cond) * (near - center)
    return center + time_step * change

def restrict(field):
    samples, rows_x, rows_y, rows_z = field.shape
    blocks = field.reshape(samples, rows_x // RF, RF, rows_y // RF, RF, rows_z // RF, RF)
    return lax.optimization_barrier(jnp.mean(blocks, axis=(2, 4, 6)))

def reference(initial_heat, cond_level, cond_table, lift_weight, lift_bias, mix_weight, mix_bias, proj_weight, spectral_weight, target_field):

    def evolve(inputs):
        field, level = inputs
        cond = jnp.take(cond_table, level)
        cond_pad = jnp.pad(cond[None], ((0, 0), (1, 1), (1, 1), (0, 0)))
        field = field[None]
        for step in range(STEPS):
            field = heat_step(jnp.pad(field, ((0, 0), (1, 1), (1, 1), (0, 0))), cond_pad)
        return (restrict(field)[0], restrict(cond[None])[0])
    coarse_heat, coarse_cond = lax.map(evolve, (initial_heat, cond_level))
    cos_z, sin_z = dft_tables(NC, M, False)
    cos_c, sin_c = dft_tables(NC, M, True)
    slab_rows = 4
    slab_count = NC // slab_rows

    def lift(first):
        heat_slab = lax.dynamic_slice_in_dim(coarse_heat, first, slab_rows, 1)
        cond_slab = lax.dynamic_slice_in_dim(coarse_cond, first, slab_rows, 1)
        inner = lift_weight[0][:, None, None, None, None] * heat_slab[None] + lift_weight[1][:, None, None, None, None] * cond_slab[None] + lift_bias[:, None, None, None, None]
        return jax.nn.gelu(inner)

    def partial_modes(field, first):
        real_z = jnp.einsum('cbsyz,zm->cbsym', field, cos_z, precision=highest) / NC
        imag_z = -jnp.einsum('cbsyz,zm->cbsym', field, sin_z, precision=highest) / NC
        real_y = (jnp.einsum('cbsym,yk->cbskm', real_z, cos_c, precision=highest) + jnp.einsum('cbsym,yk->cbskm', imag_z, sin_c, precision=highest)) / NC
        imag_y = (jnp.einsum('cbsym,yk->cbskm', imag_z, cos_c, precision=highest) - jnp.einsum('cbsym,yk->cbskm', real_z, sin_c, precision=highest)) / NC
        cos_x = lax.dynamic_slice_in_dim(cos_c, first, slab_rows, 0)
        sin_x = lax.dynamic_slice_in_dim(sin_c, first, slab_rows, 0)
        real_x = (jnp.einsum('cbskm,sj->cbjkm', real_y, cos_x, precision=highest) + jnp.einsum('cbskm,sj->cbjkm', imag_y, sin_x, precision=highest)) / NC
        imag_x = (jnp.einsum('cbskm,sj->cbjkm', imag_y, cos_x, precision=highest) - jnp.einsum('cbskm,sj->cbjkm', real_y, sin_x, precision=highest)) / NC
        return jnp.stack([real_x, imag_x])
    empty = jnp.zeros((2, C, B, M, M, M), jnp.float32)

    def first_pass(carry, slab_index):
        first = slab_index * slab_rows
        return (carry + partial_modes(lift(first), first), None)
    slab_indices = jnp.arange(slab_count, dtype=jnp.int32)
    modes_in, unused = lax.scan(first_pass, empty, slab_indices)
    weights = spectral_weight.reshape(M, M, M, 2, C, C)
    mixed_real = jnp.einsum('mkjio,ibjkm->objkm', weights[:, :, :, 0], modes_in[0], precision=highest) - jnp.einsum('mkjio,ibjkm->objkm', weights[:, :, :, 1], modes_in[1], precision=highest)
    mixed_imag = jnp.einsum('mkjio,ibjkm->objkm', weights[:, :, :, 0], modes_in[1], precision=highest) + jnp.einsum('mkjio,ibjkm->objkm', weights[:, :, :, 1], modes_in[0], precision=highest)

    def spectral_slab(first):
        cos_x = lax.dynamic_slice_in_dim(cos_c, first, slab_rows, 0)
        sin_x = lax.dynamic_slice_in_dim(sin_c, first, slab_rows, 0)
        real_x = jnp.einsum('objkm,sj->obskm', mixed_real, cos_x, precision=highest) - jnp.einsum('objkm,sj->obskm', mixed_imag, sin_x, precision=highest)
        imag_x = jnp.einsum('objkm,sj->obskm', mixed_imag, cos_x, precision=highest) + jnp.einsum('objkm,sj->obskm', mixed_real, sin_x, precision=highest)
        real_y = jnp.einsum('obskm,yk->obsym', real_x, cos_c, precision=highest) - jnp.einsum('obskm,yk->obsym', imag_x, sin_c, precision=highest)
        imag_y = jnp.einsum('obskm,yk->obsym', imag_x, cos_c, precision=highest) + jnp.einsum('obskm,yk->obsym', real_x, sin_c, precision=highest)
        return jnp.einsum('obsym,zm->obsyz', real_y, cos_z, precision=highest) - jnp.einsum('obsym,zm->obsyz', imag_y, sin_z, precision=highest)

    def second_pass(carry, slab_index):
        first = slab_index * slab_rows
        lifted = lift(first)
        before = jnp.einsum('io,ibsyz->obsyz', mix_weight, lifted, precision=highest) + mix_bias[:, None, None, None, None] + spectral_slab(first)
        activated, pullback = jax.vjp(jax.nn.gelu, before)
        slope = pullback(jnp.ones_like(before))[0]
        predicted = jnp.einsum('o,obsyz->bsyz', proj_weight, activated, precision=highest)
        target_slab = lax.dynamic_slice_in_dim(target_field, first, slab_rows, 1)
        source = slope * proj_weight[:, None, None, None, None] * (predicted - target_slab)[None]
        return (carry + partial_modes(source, first), predicted)
    modes_out, slabs = lax.scan(second_pass, empty, slab_indices)
    prediction = jnp.moveaxis(slabs, 0, 1).reshape(B, NC, NC, NC)
    grad_real = jnp.einsum('objkm,ibjkm->mkjio', modes_out[0], modes_in[0], precision=highest) + jnp.einsum('objkm,ibjkm->mkjio', modes_out[1], modes_in[1], precision=highest)
    grad_imag = jnp.einsum('objkm,ibjkm->mkjio', modes_out[1], modes_in[0], precision=highest) - jnp.einsum('objkm,ibjkm->mkjio', modes_out[0], modes_in[1], precision=highest)
    spectral_grad = (jnp.stack([grad_real, grad_imag], axis=3) / B).reshape(KZB, PAIRS, M, 2, C, C)
    return (prediction, spectral_grad)
```

```python
import math

import jax
import jax.numpy as jnp
import numpy as np
from jax import lax
from jax.experimental import pallas as pl
from jax.experimental.pallas import tpu as pltpu
from jax.sharding import PartitionSpec as P

f32 = jnp.float32
bf16 = jnp.bfloat16
highest = lax.Precision.HIGHEST

M = 16
NC = 128
FN = 256
STEPS = 4
TILES = 32
SUBS = 8
DEVICES = TILES * SUBS
CH = 32
BX = 256
YZ = 2048
VMEM = 48 * 1024 * 1024
NT = (((1,), (1,)), ((), ()))
NN = (((1,), (0,)), ((), ()))
SQRT_2_PI = math.sqrt(2.0 / math.pi)


def freq(k):
    return np.where(k >= M // 2, k - M, k)


def split_np(table):
    hi = table.astype(jnp.bfloat16)
    lo = (table - hi.astype(np.float64)).astype(jnp.bfloat16)
    return hi, lo


def plane_table():
    row = np.arange(2 * DEVICES)
    dest = 4 * (row // 8) + np.array([0, 0, 2, 2, 1, 1, 3, 3])[row % 8]
    imag = row % 2
    pair, block = dest // SUBS, dest % SUBS
    ky = freq(pair % M)
    kz = 2 * block + pair // M
    y = np.repeat(np.arange(16), NC)
    z = np.tile(np.arange(NC), 16)
    cycles = (ky[:, None] * y[None] + kz[:, None] * z[None]) % NC
    angle = cycles * (2.0 * math.pi / NC)
    return split_np(np.where(imag[:, None] == 1, -np.sin(angle), np.cos(angle)))


def line_tables():
    k = np.arange(M)
    xp, kx, ro = [v.reshape(-1) for v in np.meshgrid(np.arange(2), k, np.arange(2), indexing="ij")]
    t, _, h, ri = [
        v.reshape(-1)
        for v in np.meshgrid(np.arange(TILES), np.arange(2), np.arange(2), np.arange(2), indexing="ij")
    ]
    x = 4 * t[None] + 2 * h[None] + xp[:, None]
    angle = (freq(kx)[:, None] * x % NC) * (2.0 * math.pi / NC)
    sign = np.where(ro == 0, 1.0, -1.0)[:, None]
    fwd = np.where(ro[:, None] == ri[None], np.cos(angle), sign * np.sin(angle)) / NC**3
    t, h, ro = [
        v.reshape(-1) for v in np.meshgrid(np.arange(TILES), np.arange(2), np.arange(2), indexing="ij")
    ]
    xp, _, kx, ri = [
        v.reshape(-1)
        for v in np.meshgrid(np.arange(2), np.arange(2), k, np.arange(2), indexing="ij")
    ]
    x = 4 * t[:, None] + 2 * h[:, None] + xp[None]
    angle = (freq(kx)[None] * x % NC) * (2.0 * math.pi / NC)
    sign = np.where(ro == 0, -1.0, 1.0)[:, None]
    inv = np.where(ro[:, None] == ri[None], np.cos(angle), sign * np.sin(angle))
    return split_np(fwd) + split_np(inv)


def phase_table():
    angle = (np.arange(SUBS)[:, None] * freq(np.arange(M))[None] % SUBS) * (2.0 * math.pi / SUBS)
    return np.concatenate([np.cos(angle), np.sin(angle)], axis=1).reshape(-1).astype(np.float32)


def split(value):
    hi = value.astype(bf16)
    return hi, (value - hi.astype(f32)).astype(bf16)


def dot(a, b, dims):
    return lax.dot_general(a, b, dims, preferred_element_type=f32)


def dot3(a, b, dims):
    return dot(a[0], b[0], dims) + (dot(a[1], b[0], dims) + dot(a[0], b[1], dims))


def row_iota(shape):
    return lax.broadcasted_iota(jnp.int32, shape, 0)


def lane_iota(shape):
    return lax.broadcasted_iota(jnp.int32, shape, 1)


def swap_rows(value):
    rows = value.shape[0]
    return jnp.where(
        row_iota(value.shape) % 2 == 0, pltpu.roll(value, rows - 1, 0), pltpu.roll(value, 1, 0)
    )


def gelu_parts(v):
    square = v * v
    t = jnp.tanh(SQRT_2_PI * (v + 0.044715 * (square * v)))
    half = 0.5 + 0.5 * t
    return square, t, half


def lift_rows(g, y, heat_ref, cond_ref, lift_ref):
    heat = heat_ref[g, y : y + 1, :]
    cond = cond_ref[g, y : y + 1, :]
    v = lift_ref[0] * heat + lift_ref[1] * cond + lift_ref[2]
    return v * gelu_parts(v)[2]


def store_lifted(heat_ref, cond_ref, lift_ref, hi_ref, lo_ref):
    def group(g, carry):
        rows = pl.ds(pl.multiple_of(g * CH, CH), CH)
        for y in range(16):
            hi, lo = split(lift_rows(g, y, heat_ref, cond_ref, lift_ref))
            hi_ref[rows, y * NC : (y + 1) * NC] = hi
            lo_ref[rows, y * NC : (y + 1) * NC] = lo
        return carry

    lax.fori_loop(0, 8, group, 0)


def send_modes(hi_ref, lo_ref, table_hi_ref, table_lo_ref, phase_ref, sub, out_ref):
    for part in range(4):
        rows = slice(128 * part, 128 * part + 128)
        t_hi, t_lo = table_hi_ref[rows, :], table_lo_ref[rows, :]
        hi, lo = hi_ref[...], lo_ref[...]
        modes = dot(t_hi, hi, NT) + (dot(t_lo, hi, NT) + dot(t_hi, lo, NT))
        sign = jnp.where(row_iota((8, NC)) % 2 == 0, 1.0, -1.0).astype(f32)
        keep = row_iota((8, NC)) % 4 < 2
        for tile in range(16):
            j = 16 * part + tile
            ky = (j // 2) % M
            cos = phase_ref[sub * 32 + ky]
            sin = phase_ref[sub * 32 + 16 + ky]
            halves = []
            for h in range(2):
                v = modes[8 * tile : 8 * tile + 8, h * NC : (h + 1) * NC]
                halves.append(v * cos + swap_rows(v) * (sign * sin))
            first, second = halves
            out_ref[16 * j : 16 * j + 8, :] = jnp.where(keep, first, pltpu.roll(second, 2, 0))
            out_ref[16 * j + 8 : 16 * j + 16, :] = jnp.where(keep, pltpu.roll(first, 6, 0), second)


def heat_kernel(
    heat_ref,
    level_ref,
    xup_ref,
    xdn_ref,
    yup_ref,
    ydn_ref,
    levels_ref,
    lift_ref,
    pair_ref,
    phase_ref,
    table_hi_hbm,
    table_lo_hbm,
    coarse_heat_ref,
    coarse_cond_ref,
    out_ref,
    h_ref,
    c_ref,
    kx_ref,
    ky_ref,
    kz_ref,
    mask_ref,
    sum_ref,
    half_ref,
    hi_ref,
    lo_ref,
    table_hi_ref,
    table_lo_ref,
    sem,
):
    copies = [
        pltpu.make_async_copy(table_hi_hbm, table_hi_ref, sem.at[0]),
        pltpu.make_async_copy(table_lo_hbm, table_lo_ref, sem.at[1]),
    ]
    for copy in copies:
        copy.start()
    tile = lax.axis_index("tile")
    sub = lax.axis_index("sub")
    shape = (40, FN)
    row = row_iota(shape)
    lane = lane_iota(shape)
    outside = ((row >= 32) & (row < 36) & (sub == SUBS - 1)) | ((row >= 36) & (sub == 0))
    inside = jnp.where(outside, 0.0, 1.0).astype(f32)
    mask_ref[0] = inside * jnp.where(tile == 0, 0.0, 1.0).astype(f32)
    mask_ref[1] = inside
    mask_ref[2] = inside * jnp.where(tile == TILES - 1, 0.0, 1.0).astype(f32)

    def lookup(level):
        bits = [(level & (1 << i)) != 0 for i in range(4)]
        values = [levels_ref[i] for i in range(16)]
        for bit in bits:
            values = [
                jnp.where(bit, values[2 * i + 1], values[2 * i]) for i in range(len(values) // 2)
            ]
        return values[0]

    for b in range(2):
        for i in range(4):
            h_ref[b, i] = xup_ref[0, b, i]
            h_ref[b, 12 + i] = xdn_ref[0, b, i]
        for i in range(8):
            h_ref[b, 4 + i, 0:32] = heat_ref[b, i]
            h_ref[b, 4 + i, 32:36] = ydn_ref[0, b, i]
            h_ref[b, 4 + i, 36:40] = yup_ref[0, b, i]

    def cond_low(i, carry):
        for b in range(2):
            c_ref[b, i] = lookup(xup_ref[1, b, i].astype(jnp.int32)) * mask_ref[0]
            c_ref[b, 12 + i] = lookup(xdn_ref[1, b, i].astype(jnp.int32)) * mask_ref[2]
        return carry

    lax.fori_loop(0, 4, cond_low, 0)

    def cond_mid(i, carry):
        for b in range(2):
            c_ref[b, 4 + i, 0:32] = lookup(level_ref[b, i])
            c_ref[b, 4 + i, 32:36] = lookup(ydn_ref[1, b, i].astype(jnp.int32)) * mask_ref[1, 32:36]
            c_ref[b, 4 + i, 36:40] = lookup(yup_ref[1, b, i].astype(jnp.int32)) * mask_ref[1, 36:40]
        return carry

    lax.fori_loop(0, 8, cond_mid, 0)

    last = lane == FN - 1
    first = lane == 0

    def faces(i, carry):
        for b in range(2):
            c = c_ref[b, i] * 0.08
            kx_ref[b, i] = c + c_ref[b, i + 1] * 0.08
            ky_ref[b, i] = c + pltpu.roll(c, 39, 0)
            kz_ref[b, i] = c + jnp.where(last, 0.0, pltpu.roll(c, FN - 1, 1))
        return carry

    lax.fori_loop(0, 15, faces, 0)

    for step in range(1, STEPS + 1):
        for b in range(2):

            def layer(i, flow_x):
                h = h_ref[b, i]
                next_x = kx_ref[b, i] * (h_ref[b, i + 1] - h)
                flow_y = ky_ref[b, i] * (pltpu.roll(h, 39, 0) - h)
                flow_z = kz_ref[b, i] * (jnp.where(last, 0.0, pltpu.roll(h, FN - 1, 1)) - h)
                low_z = jnp.where(first, (0.08 * c_ref[b, i]) * h, pltpu.roll(flow_z, 1, 1))
                change = (next_x - flow_x) + (flow_y - pltpu.roll(flow_y, 1, 0)) + (flow_z - low_z)
                which = jnp.where(i >= 4, 1, 0) + jnp.where(i >= 12, 1, 0)
                h_ref[b, i] = h + mask_ref[which] * change
                return next_x

            start = kx_ref[b, step - 1] * (h_ref[b, step] - h_ref[b, step - 1])
            lax.fori_loop(step, 16 - step, layer, start)

    for b in range(2):
        for x in range(4):
            at = 64 * (2 * x + b)
            half_ref[at : at + 32] = h_ref[b, 4 + 2 * x, 0:32] + h_ref[b, 5 + 2 * x, 0:32]
            half_ref[at + 32 : at + 64] = c_ref[b, 4 + 2 * x, 0:32] + c_ref[b, 5 + 2 * x, 0:32]
    sum_ref[...] = lax.dot_general(
        half_ref[...], pair_ref[...], NN, precision=highest, preferred_element_type=f32
    )
    for g in range(8):
        for at, target in ((64 * g, coarse_heat_ref), (64 * g + 32, coarse_cond_ref)):
            target[g] = (
                sum_ref[pl.ds(at, 16, stride=2), :] + sum_ref[pl.ds(at + 1, 16, stride=2), :]
            )

    store_lifted(coarse_heat_ref, coarse_cond_ref, lift_ref, hi_ref, lo_ref)
    for copy in copies:
        copy.wait()
    send_modes(hi_ref, lo_ref, table_hi_ref, table_lo_ref, phase_ref, sub, out_ref)


def line_modes(in_ref, fwd_hi_ref, fwd_lo_ref):
    sums = []
    for t in range(TILES):
        rows = [in_ref[32 * t + 8 * i : 32 * t + 8 * i + 8, :] for i in range(4)]
        sums.append((rows[0] + rows[1]) + (rows[2] + rows[3]))
    received = split(jnp.concatenate(sums, axis=0))
    both = dot3((fwd_hi_ref[...], fwd_lo_ref[...]), received, NN)
    modes = both[0:32] + pltpu.roll(both[32:64], 64, 1)
    return jnp.concatenate([modes, pltpu.roll(modes, 96, 1)], axis=0)


def mix_kernel(
    in_ref, weight_ref, fwd_hi_ref, fwd_lo_ref, inv_hi_ref, inv_lo_ref, modes_ref, out_ref, w_ref
):
    for kx in range(M):
        for ri in range(2):
            at = kx * 64 + ri * 32
            w_ref[:, at : at + 32] = weight_ref[kx, ri]
    modes = line_modes(in_ref, fwd_hi_ref, fwd_lo_ref)
    modes_ref[...] = modes
    spread = dot3(split(modes[:, 0:32]), split(w_ref[...]), NN)
    shape = (64, NC)
    own = (row_iota(shape) % 32) // 2
    side = lane_iota(shape) // 64
    total = jnp.zeros(shape, f32)
    for part in range(8):
        total = total + jnp.where(own == 2 * part + side, spread[:, part * NC : (part + 1) * NC], 0.0)
    total = total + pltpu.roll(total, 64, 1)
    sign = jnp.where(row_iota(shape) % 2 == 0, -1.0, 1.0).astype(f32)
    mixed = total + sign * swap_rows(pltpu.roll(total, 96, 1))
    mixed = jnp.where(lane_iota(shape) < 32, mixed, 0.0)
    mixed = mixed + pltpu.roll(mixed, 32, 1)
    mixed = mixed + pltpu.roll(mixed, 64, 1)
    mixed = jnp.concatenate([mixed, mixed], axis=0)
    square = (NC, NC)
    mixed = jnp.where(row_iota(square) // 32 == lane_iota(square) // 32, mixed, 0.0)
    lines = dot3((inv_hi_ref[...], inv_lo_ref[...]), split(mixed), NN)
    upper = row_iota((8, NC)) < 4
    for pair in range(16):
        v = lines[8 * pair : 8 * pair + 8]
        turned = pltpu.roll(v, 4, 0)
        for odd, value in enumerate((jnp.where(upper, v, turned), jnp.where(upper, turned, v))):
            for copy in range(4):
                at = (2 * pair + odd) * 32 + 8 * copy
                out_ref[at : at + 8, :] = value


def field_kernel(
    in_ref,
    coarse_heat_ref,
    coarse_cond_ref,
    target_ref,
    lift_ref,
    point_ref,
    layer_ref,
    phase_ref,
    table_hi_hbm,
    table_lo_hbm,
    prediction_ref,
    out_ref,
    v_ref,
    before_ref,
    hi_ref,
    lo_ref,
    table_hi_ref,
    table_lo_ref,
    sem,
):
    copies = [
        pltpu.make_async_copy(table_hi_hbm, table_hi_ref, sem.at[0]),
        pltpu.make_async_copy(table_lo_hbm, table_lo_ref, sem.at[1]),
    ]
    for copy in copies:
        copy.start()
    sub = lax.axis_index("sub")
    store_lifted(coarse_heat_ref, coarse_cond_ref, lift_ref, hi_ref, lo_ref)
    sign = jnp.where(row_iota((8, NC)) % 2 == 0, -1.0, 1.0).astype(f32)
    keep = row_iota((8, NC)) % 4 < 2
    for j in range(64):
        ky = (j // 2) % M
        cos = phase_ref[sub * 32 + ky]
        sin = phase_ref[sub * 32 + 16 + ky]
        first = in_ref[16 * j : 16 * j + 8, :]
        second = in_ref[16 * j + 8 : 16 * j + 16, :]
        low = jnp.where(keep, first, pltpu.roll(second, 2, 0))
        high = jnp.where(keep, pltpu.roll(first, 6, 0), second)
        for h, v in enumerate((low, high)):
            v_ref[8 * j : 8 * j + 8, h * NC : (h + 1) * NC] = v * cos + swap_rows(v) * (sign * sin)
    modes = split(jnp.transpose(v_ref[...]))
    square = (BX, BX)
    own = row_iota(square) // CH == lane_iota(square) // CH
    point = split(jnp.where(own, point_ref[...], 0.0))
    for copy in copies:
        copy.wait()

    def chunk(i, carry):
        cols = pl.ds(pl.multiple_of(i * 256, 256), 256)
        before_ref[...] = dot3(point, (hi_ref[:, cols], lo_ref[:, cols]), NN) + dot3(
            modes, (table_hi_ref[:, cols], table_lo_ref[:, cols]), NN
        )
        for g in range(8):
            for q in range(2):
                y = 2 * i + q
                v = before_ref[32 * g : 32 * g + 32, q * NC : (q + 1) * NC] + layer_ref[0]
                square, t, half = gelu_parts(v)
                predicted = jnp.sum(layer_ref[1] * (v * half), axis=0, keepdims=True)
                x, b = g // 2, g % 2
                prediction_ref[b, x, pl.ds(y, 1), :] = predicted
                miss = predicted - target_ref[b, x, pl.ds(y, 1), :]
                slope = half + (0.5 * SQRT_2_PI) * v * (1.0 - t * t) * (1.0 + 0.134145 * square)
                hi, lo = split(slope * layer_ref[1] * miss)
                at = pl.ds(pl.multiple_of(i * 256 + q * NC, NC), NC)
                hi_ref[32 * g : 32 * g + 32, at] = hi
                lo_ref[32 * g : 32 * g + 32, at] = lo
        return carry

    lax.fori_loop(0, 8, chunk, 0)
    send_modes(hi_ref, lo_ref, table_hi_ref, table_lo_ref, phase_ref, sub, out_ref)


def grad_kernel(in_ref, modes_ref, fwd_hi_ref, fwd_lo_ref, out_ref):
    modes_out = line_modes(in_ref, fwd_hi_ref, fwd_lo_ref)
    shape = (64, NC)
    sign = jnp.where(row_iota(shape) % 2 == 0, 1.0, -1.0).astype(f32)
    turned = sign * swap_rows(modes_out)
    right = jnp.where(lane_iota(shape) < 32, modes_out, pltpu.roll(turned, 32, 1))
    left = jnp.transpose(modes_ref[...])[0:32]
    left = jnp.concatenate([left] * M, axis=0) * 0.5
    wide = (32 * M, 64)
    own = row_iota(wide) // 32 == (lane_iota(wide) % 32) // 2
    left = jnp.where(own, left, 0.0)
    grads = dot3(split(left), split(right), NN)
    for kx in range(M):
        block = grads[32 * kx : 32 * kx + 32]
        out_ref[kx, 0] = block[:, 0:32]
        out_ref[kx, 1] = pltpu.roll(block, 96, 1)[:, 0:32]


def vmem():
    return pl.BlockSpec(memory_space=pltpu.VMEM)


def smem():
    return pl.BlockSpec(memory_space=pltpu.SMEM)


def hbm():
    return pl.BlockSpec(memory_space=pl.ANY)


def params():
    return pltpu.CompilerParams(vmem_limit_bytes=VMEM)


def exchange(block):
    return lax.all_to_all(
        block.reshape(DEVICES, 4, NC), ("tile", "sub"), split_axis=0, concat_axis=0, tiled=True
    ).reshape(4 * DEVICES, NC)


def shifted(block, axis, up):
    count = lax.axis_size(axis)
    pairs = [(i, i + 1) if up else (i + 1, i) for i in range(count - 1)]
    return lax.ppermute(block, axis, pairs)


def local(
    initial_heat,
    cond_level,
    cond_table,
    lift_weight,
    lift_bias,
    mix_weight,
    mix_bias,
    proj_weight,
    spectral_weight,
    target_field,
):
    table_hi, table_lo = [jnp.asarray(v) for v in plane_table()]
    fwd_hi, fwd_lo, inv_hi, inv_lo = [jnp.asarray(v) for v in line_tables()]
    phase = jnp.asarray(phase_table())
    pair = np.zeros((FN, NC), np.float32)
    pair[np.arange(FN), np.arange(FN) // 2] = 0.125

    with jax.named_scope("halo"):
        fields = (initial_heat, cond_level.astype(f32))
        yup = shifted(jnp.stack([v[:, :, 28:] for v in fields]), "sub", True)
        ydn = shifted(jnp.stack([v[:, :, :4] for v in fields]), "sub", False)

        def layers(at):
            return jnp.stack(
                [
                    jnp.concatenate(
                        [v[:, at : at + 4], ydn[i][:, at : at + 4], yup[i][:, at : at + 4]], axis=2
                    )
                    for i, v in enumerate(fields)
                ]
            )

        xup = shifted(layers(4), "tile", True)
        xdn = shifted(layers(0), "tile", False)

    lift = jnp.broadcast_to(
        jnp.concatenate([lift_weight, lift_bias[None]], axis=0)[:, :, None], (3, CH, NC)
    )
    layer = jnp.broadcast_to(jnp.stack([mix_bias, proj_weight])[:, :, None], (2, CH, NC))
    point = jnp.tile(mix_weight.T, (8, 8))

    coarse = jax.ShapeDtypeStruct((8, 16, NC), f32)
    blocks = jax.ShapeDtypeStruct((4 * DEVICES, NC), f32)
    grid_shape = (2, 16, 40, FN)
    tables = [pltpu.VMEM((2 * DEVICES, YZ), bf16)] * 2 + [pltpu.SemaphoreType.DMA((2,))]
    with jax.named_scope("heat"):
        coarse_heat, coarse_cond, block = pl.pallas_call(
            heat_kernel,
            out_shape=(coarse, coarse, blocks),
            in_specs=[vmem()] * 6 + [smem(), vmem(), vmem(), smem(), hbm(), hbm()],
            out_specs=(vmem(),) * 3,
            scratch_shapes=[pltpu.VMEM(grid_shape, f32)] * 5
            + [
                pltpu.VMEM((3, 40, FN), f32),
                pltpu.VMEM((512, NC), f32),
                pltpu.VMEM((512, FN), f32),
                pltpu.VMEM((BX, YZ), bf16),
                pltpu.VMEM((BX, YZ), bf16),
            ]
            + tables,
            compiler_params=params(),
        )(
            initial_heat,
            cond_level,
            xup,
            xdn,
            yup,
            ydn,
            cond_table,
            lift,
            jnp.asarray(pair),
            phase,
            table_hi,
            table_lo,
        )
    block = exchange(block)
    with jax.named_scope("mix"):
        modes_in, block = pl.pallas_call(
            mix_kernel,
            out_shape=(jax.ShapeDtypeStruct((64, NC), f32), blocks),
            in_specs=[vmem()] * 6,
            out_specs=(vmem(),) * 2,
            scratch_shapes=[pltpu.VMEM((CH, 64 * M), f32)],
            compiler_params=params(),
        )(block, spectral_weight.reshape(M, 2, CH, CH), fwd_hi, fwd_lo, inv_hi, inv_lo)
    block = exchange(block)
    with jax.named_scope("field"):
        prediction, block = pl.pallas_call(
            field_kernel,
            out_shape=(jax.ShapeDtypeStruct(target_field.shape, f32), blocks),
            in_specs=[vmem()] * 7 + [smem(), hbm(), hbm()],
            out_specs=(vmem(),) * 2,
            scratch_shapes=[
                pltpu.VMEM((2 * DEVICES, BX), f32),
                pltpu.VMEM((BX, 256), f32),
                pltpu.VMEM((BX, YZ), bf16),
                pltpu.VMEM((BX, YZ), bf16),
            ]
            + tables,
            compiler_params=params(),
        )(
            block,
            coarse_heat,
            coarse_cond,
            target_field,
            lift,
            point,
            layer,
            phase,
            table_hi,
            table_lo,
        )
    block = exchange(block)
    with jax.named_scope("grad"):
        spectral_grad = pl.pallas_call(
            grad_kernel,
            out_shape=jax.ShapeDtypeStruct((M, 2, CH, CH), f32),
            in_specs=[vmem()] * 4,
            out_specs=vmem(),
            compiler_params=params(),
        )(block, modes_in, fwd_hi, fwd_lo)
    return (prediction, spectral_grad.reshape(1, 1, M, 2, CH, CH))


def solution(mesh):
    in_specs = (
        P(None, "tile", "sub", None),
        P(None, "tile", "sub", None),
        P(),
        P(),
        P(),
        P(),
        P(),
        P(),
        P("sub", "tile", None, None, None, None),
        P(None, "tile", "sub", None),
    )
    out_specs = (P(None, "tile", "sub", None), P("sub", "tile", None, None, None, None))
    return jax.shard_map(local, mesh=mesh, in_specs=in_specs, out_specs=out_specs, check_vma=False)
```

```python
import math

import jax
import jax.numpy as jnp
import numpy as np
from jax import lax
from jax.experimental import pallas as pl
from jax.experimental.pallas import tpu as pltpu
from jax.sharding import PartitionSpec as P

f32 = jnp.float32
bf16 = jnp.bfloat16
highest = lax.Precision.HIGHEST

M = 16
NC = 128
FN = 256
STEPS = 4
TILES = 32
SUBS = 8
DEVICES = TILES * SUBS
CH = 32
BX = 256
YZ = 2048
NT = (((1,), (1,)), ((), ()))
NN = (((1,), (0,)), ((), ()))
SQRT_2_PI = math.sqrt(2.0 / math.pi)


def freq(k):
    return np.where(k >= M // 2, k - M, k)


def split_np(table):
    hi = table.astype(jnp.bfloat16)
    lo = (table - hi.astype(np.float64)).astype(jnp.bfloat16)
    return hi, lo


def stacked_np(table):
    return np.concatenate(split_np(table), axis=0)


def plane_table():
    row = np.arange(2 * DEVICES)
    dest = 4 * (row // 8) + np.array([0, 0, 2, 2, 1, 1, 3, 3])[row % 8]
    imag = row % 2
    pair, block = dest // SUBS, dest % SUBS
    ky = freq(pair % M)
    kz = 2 * block + pair // M
    y = np.repeat(np.arange(16), NC)
    z = np.tile(np.arange(NC), 16)
    cycles = (ky[:, None] * y[None] + kz[:, None] * z[None]) % NC
    angle = cycles * (2.0 * math.pi / NC)
    return stacked_np(np.where(imag[:, None] == 1, -np.sin(angle), np.cos(angle)))


def line_tables():
    k = np.arange(M)
    xp, kx, ro = [v.reshape(-1) for v in np.meshgrid(np.arange(2), k, np.arange(2), indexing="ij")]
    t, _, h, ri = [
        v.reshape(-1)
        for v in np.meshgrid(np.arange(TILES), np.arange(2), np.arange(2), np.arange(2), indexing="ij")
    ]
    x = 4 * t[None] + 2 * h[None] + xp[:, None]
    angle = (freq(kx)[:, None] * x % NC) * (2.0 * math.pi / NC)
    sign = np.where(ro == 0, 1.0, -1.0)[:, None]
    fwd = np.where(ro[:, None] == ri[None], np.cos(angle), sign * np.sin(angle)) / NC**3
    t, h, ro = [
        v.reshape(-1) for v in np.meshgrid(np.arange(TILES), np.arange(2), np.arange(2), indexing="ij")
    ]
    xp, _, kx, ri = [
        v.reshape(-1)
        for v in np.meshgrid(np.arange(2), np.arange(2), k, np.arange(2), indexing="ij")
    ]
    x = 4 * t[:, None] + 2 * h[:, None] + xp[None]
    angle = (freq(kx)[None] * x % NC) * (2.0 * math.pi / NC)
    sign = np.where(ro == 0, -1.0, 1.0)[:, None]
    inv = np.where(ro[:, None] == ri[None], np.cos(angle), sign * np.sin(angle))
    return split_np(fwd) + split_np(inv)


def phase(sub, pair):
    turn = int(freq(np.array(pair % M))) * sub

    def cosine(k):
        k = k & 7
        half = math.sqrt(0.5)
        near = jnp.where(k == 0, 1.0, jnp.where((k == 1) | (k == 7), half, 0.0))
        return jnp.where(k == 4, -1.0, jnp.where((k == 3) | (k == 5), -half, near)).astype(f32)

    return cosine(turn), cosine(turn + 6)


def split(value):
    hi = value.astype(bf16)
    return hi, (value - hi.astype(f32)).astype(bf16)


def dot(a, b, dims):
    return lax.dot_general(a, b, dims, preferred_element_type=f32)


def dot3(a, b, dims):
    return dot(a[0], b[0], dims) + (dot(a[1], b[0], dims) + dot(a[0], b[1], dims))


def row_iota(shape):
    return lax.broadcasted_iota(jnp.int32, shape, 0)


def lane_iota(shape):
    return lax.broadcasted_iota(jnp.int32, shape, 1)


def swap_rows(value):
    rows = value.shape[0]
    return jnp.where(
        row_iota(value.shape) % 2 == 0, pltpu.roll(value, rows - 1, 0), pltpu.roll(value, 1, 0)
    )


def gelu_parts(v):
    square = v * v
    t = jnp.tanh(SQRT_2_PI * (v + 0.044715 * (square * v)))
    half = 0.5 + 0.5 * t
    return square, t, half


def lift_rows(g, y, heat_ref, cond_ref, lift_ref):
    heat = heat_ref[g, y : y + 1, :]
    cond = cond_ref[g, y : y + 1, :]
    v = lift_ref[0] * heat + lift_ref[1] * cond + lift_ref[2]
    return v * gelu_parts(v)[2]


def store_lifted(heat_ref, cond_ref, lift_ref, hi_ref, lo_ref):
    def group(g, carry):
        rows = pl.ds(pl.multiple_of(g * CH, CH), CH)
        for y in range(16):
            hi, lo = split(lift_rows(g, y, heat_ref, cond_ref, lift_ref))
            hi_ref[rows, y * NC : (y + 1) * NC] = hi
            lo_ref[rows, y * NC : (y + 1) * NC] = lo
        return carry

    lax.fori_loop(0, 8, group, 0, unroll=True)


def send_modes(hi_ref, lo_ref, table_ref, sub, out_ref):
    rows = 2 * DEVICES
    both = dot(table_ref[...], hi_ref[...], NT)
    modes = both[:rows] + (both[rows:] + dot(table_ref[:rows], lo_ref[...], NT))
    sign = jnp.where(row_iota((8, NC)) % 2 == 0, 1.0, -1.0).astype(f32)
    keep = row_iota((8, NC)) % 4 < 2
    for j in range(64):
        cos, sin = phase(sub, j // 2)
        halves = []
        for h in range(2):
            v = modes[8 * j : 8 * j + 8, h * NC : (h + 1) * NC]
            halves.append(v * cos + swap_rows(v) * (sign * sin))
        first, second = halves
        out_ref[16 * j : 16 * j + 8, :] = jnp.where(keep, first, pltpu.roll(second, 2, 0))
        out_ref[16 * j + 8 : 16 * j + 16, :] = jnp.where(keep, pltpu.roll(first, 6, 0), second)


def pack_kernel(
    heat_hbm,
    level_hbm,
    heat_b_ref,
    level_b_ref,
    ya_ref,
    yb_ref,
    heat_a_ref,
    level_a_ref,
    heat_ref,
    level_ref,
    sem,
):
    copies = [
        pltpu.make_async_copy(heat_hbm, heat_ref, sem.at[0]),
        pltpu.make_async_copy(level_hbm, level_ref, sem.at[1]),
    ]
    for copy in copies:
        copy.start()
    at_a = jnp.where(lax.axis_index("tile") % 2 == 0, 4, 0)
    at_b = 4 - at_a
    even = lax.axis_index("sub") % 2 == 0
    for copy in copies:
        copy.wait()
    for b in range(2):
        for i in range(4):
            heat_b_ref[b, i] = heat_ref[b, at_b + i]
            level_b_ref[b, i] = level_ref[b, at_b + i]
            heat_a_ref[b, i] = heat_ref[b, at_a + i]
            level_a_ref[b, i] = level_ref[b, at_a + i]
        for i in range(8):
            for f, source in enumerate((heat_ref, level_ref)):
                top = source[b, i, 28:32].astype(f32)
                low = source[b, i, 0:4].astype(f32)
                ya_ref[f, b, i] = jnp.where(even, top, low)
                yb_ref[f, b, i] = jnp.where(even, low, top)


def corner_kernel(ya_ref, yb_ref, heat_b_ref, level_b_ref, corner_b_ref, corner_a_ref):
    at_a = jnp.where(lax.axis_index("tile") % 2 == 0, 4, 0)
    for f in range(2):
        for b in range(2):
            for i in range(4):
                for at, target in ((at_a, corner_a_ref), (4 - at_a, corner_b_ref)):
                    target[f, b, i, 0:4] = ya_ref[f, b, at + i]
                    target[f, b, i, 4:8] = yb_ref[f, b, at + i]


def heat_kernel(
    heat_hbm,
    level_hbm,
    heat_a_ref,
    level_a_ref,
    heat_b_ref,
    level_b_ref,
    ya_ref,
    yb_ref,
    corner_a_ref,
    corner_b_ref,
    lift_ref,
    levels_hbm,
    table_hbm,
    out_ref,
    hi_ref,
    lo_ref,
    coarse_heat_ref,
    coarse_cond_ref,
    h_ref,
    next_ref,
    c_ref,
    d_ref,
    kx_ref,
    ky_ref,
    kyl_ref,
    kz_ref,
    kzl_ref,
    sum_ref,
    half_ref,
    level_ref,
    table_ref,
    levels_ref,
    sem,
):
    levels_copy = pltpu.make_async_copy(levels_hbm, levels_ref, sem.at[0])
    level_copy = pltpu.make_async_copy(level_hbm, level_ref, sem.at[1])
    heat_copies = [
        pltpu.make_async_copy(heat_hbm.at[b], h_ref.at[b, pl.ds(4, 8), pl.ds(0, 32)], sem.at[2 + b])
        for b in range(2)
    ]
    table_copy = pltpu.make_async_copy(table_hbm, table_ref, sem.at[4])
    for copy in [levels_copy, level_copy, *heat_copies, table_copy]:
        copy.start()
    tile = lax.axis_index("tile")
    sub = lax.axis_index("sub")
    even_tile = tile % 2 == 0
    even_sub = sub % 2 == 0
    base_a = jnp.where(even_tile, 12, 0)
    base_b = 12 - base_a
    shape = (40, FN)
    row = row_iota(shape)
    lane = lane_iota(shape)
    last = lane == FN - 1
    first = lane == 0
    top_edge = sub == SUBS - 1
    low_edge = sub == 0
    above = jnp.where(top_edge, 0.0, 1.0).astype(f32)
    below = jnp.where(low_edge, 0.0, 1.0).astype(f32)
    left = jnp.where(tile == 0, 0.0, 1.0).astype(f32)
    right = jnp.where(tile == TILES - 1, 0.0, 1.0).astype(f32)

    def lookup(level):
        bits = [(level & (1 << i)) != 0 for i in range(4)]
        values = [levels_ref[i] for i in range(16)]
        for bit in bits:
            values = [
                jnp.where(bit, values[2 * i + 1], values[2 * i]) for i in range(len(values) // 2)
            ]
        return values[0]

    eight = row_iota((8, FN))
    outer = jnp.where(eight < 4, above, below)
    levels_copy.wait()

    def outer_layers(i, carry):
        for b in range(2):
            for base, heat, level, corner, side in (
                (base_a, heat_a_ref, level_a_ref, corner_a_ref, jnp.where(even_tile, right, left)),
                (base_b, heat_b_ref, level_b_ref, corner_b_ref, jnp.where(even_tile, left, right)),
            ):
                at = base + i
                h_ref[b, at, 0:32] = heat[b, i]
                c_ref[b, at, 0:32] = lookup(level[b, i]) * side
                value = corner[0, b, i]
                h_ref[b, at, 32:40] = jnp.where(even_sub, value, pltpu.roll(value, 4, 0))
                value = corner[1, b, i]
                value = jnp.where(even_sub, value, pltpu.roll(value, 4, 0))
                c_ref[b, at, 32:40] = lookup(value.astype(jnp.int32)) * (outer * side)
        return carry

    lax.fori_loop(0, 4, outer_layers, 0)

    level_copy.wait()
    for copy in heat_copies:
        copy.wait()

    def own_layers(i, carry):
        for b in range(2):
            at = 4 + i
            c_ref[b, at, 0:32] = lookup(level_ref[b, i])
            ya = ya_ref[0, b, i]
            yb = yb_ref[0, b, i]
            h_ref[b, at, 32:36] = jnp.where(even_sub, ya, yb)
            h_ref[b, at, 36:40] = jnp.where(even_sub, yb, ya)
            ya = lookup(ya_ref[1, b, i].astype(jnp.int32))
            yb = lookup(yb_ref[1, b, i].astype(jnp.int32))
            c_ref[b, at, 32:36] = jnp.where(even_sub, ya, yb) * above
            c_ref[b, at, 36:40] = jnp.where(even_sub, yb, ya) * below
        return carry

    lax.fori_loop(0, 8, own_layers, 0, unroll=2)

    edge = ((row == 31) & top_edge) | ((row == 39) & low_edge)

    def faces(i, carry):
        for b in range(2):
            c = c_ref[b, i]
            up = pltpu.roll(c, 39, 0)
            down = pltpu.roll(c, 1, 0)
            after = jnp.where(last, 0.0, pltpu.roll(c, FN - 1, 1))
            before = jnp.where(first, 0.0, pltpu.roll(c, 1, 1))
            c_next = c_ref[b, i + 1]
            around = (c_next + c_ref[b, jnp.maximum(i - 1, 0)]) + (up + down) + (after + before)
            d_ref[b, i] = (1.0 - 0.48 * c) - 0.08 * around
            kx_ref[b, i] = 0.08 * (c + c_next)
            ky = jnp.where(edge, 0.0, 0.08 * (c + up))
            ky_ref[b, i] = ky
            kyl_ref[b, i] = pltpu.roll(ky, 1, 0)
            kz_ref[b, i] = jnp.where(last, 0.0, 0.08 * (c + after))
            kzl_ref[b, i] = jnp.where(first, 0.0, 0.08 * (c + before))
        return carry

    lax.fori_loop(0, 15, faces, 0, unroll=3)
    for b in range(2):
        kx_ref[b, 3] = kx_ref[b, 3] * left
        kx_ref[b, 11] = kx_ref[b, 11] * right

    for step in range(1, STEPS + 1):
        source, target = (h_ref, next_ref) if step % 2 == 1 else (next_ref, h_ref)

        def layer_pair(n, carry, source=source, target=target, step=step):
            for j in range(2):
                for b in range(2):
                    i = step + 2 * n + j
                    h = source[b, i]
                    along_x = kx_ref[b, i] * source[b, i + 1] + kx_ref[b, i - 1] * source[b, i - 1]
                    along_y = ky_ref[b, i] * pltpu.roll(h, 39, 0) + kyl_ref[b, i] * pltpu.roll(h, 1, 0)
                    along_z = kz_ref[b, i] * pltpu.roll(h, FN - 1, 1) + kzl_ref[b, i] * pltpu.roll(h, 1, 1)
                    target[b, i] = (d_ref[b, i] * h + along_x) + (along_y + along_z)
            return carry

        lax.fori_loop(0, 8 - step, layer_pair, 0, unroll=True)

    for b in range(2):
        for x in range(4):
            at = 64 * (2 * x + b)
            half_ref[at : at + 32] = h_ref[b, 4 + 2 * x, 0:32] + h_ref[b, 5 + 2 * x, 0:32]
            half_ref[at + 32 : at + 64] = c_ref[b, 4 + 2 * x, 0:32] + c_ref[b, 5 + 2 * x, 0:32]
    pairs = (FN, NC)
    pair = jnp.where(row_iota(pairs) // 2 == lane_iota(pairs), 0.125, 0.0).astype(f32)
    sum_ref[...] = lax.dot_general(
        half_ref[...], pair, NN, precision=highest, preferred_element_type=f32
    )
    for g in range(8):
        for at, target in ((64 * g, coarse_heat_ref), (64 * g + 32, coarse_cond_ref)):
            target[g] = (
                sum_ref[pl.ds(at, 16, stride=2), :] + sum_ref[pl.ds(at + 1, 16, stride=2), :]
            )

    store_lifted(coarse_heat_ref, coarse_cond_ref, lift_ref, hi_ref, lo_ref)
    table_copy.wait()
    send_modes(hi_ref, lo_ref, table_ref, sub, out_ref)


def line_modes(in_ref, fwd_hi_ref, fwd_lo_ref):
    sums = []
    for t in range(TILES):
        rows = [in_ref[32 * t + 8 * i : 32 * t + 8 * i + 8, :] for i in range(4)]
        sums.append((rows[0] + rows[1]) + (rows[2] + rows[3]))
    received = split(jnp.concatenate(sums, axis=0))
    both = dot3((fwd_hi_ref[...], fwd_lo_ref[...]), received, NN)
    modes = both[0:32] + pltpu.roll(both[32:64], 64, 1)
    return jnp.concatenate([modes, pltpu.roll(modes, 96, 1)], axis=0)


def mix_kernel(
    in_ref, weight_ref, fwd_hi_ref, fwd_lo_ref, inv_hi_ref, inv_lo_ref, modes_ref, out_ref, w_ref
):
    for kx in range(M):
        for ri in range(2):
            at = kx * 64 + ri * 32
            w_ref[:, at : at + 32] = weight_ref[kx, ri]
    modes = line_modes(in_ref, fwd_hi_ref, fwd_lo_ref)
    modes_ref[...] = modes
    spread = dot3(split(modes[:, 0:32]), split(w_ref[...]), NN)
    shape = (64, NC)
    own = (row_iota(shape) % 32) // 2
    side = lane_iota(shape) // 64
    total = jnp.zeros(shape, f32)
    for part in range(8):
        total = total + jnp.where(own == 2 * part + side, spread[:, part * NC : (part + 1) * NC], 0.0)
    total = total + pltpu.roll(total, 64, 1)
    sign = jnp.where(row_iota(shape) % 2 == 0, -1.0, 1.0).astype(f32)
    mixed = total + sign * swap_rows(pltpu.roll(total, 96, 1))
    mixed = jnp.where(lane_iota(shape) < 32, mixed, 0.0)
    mixed = mixed + pltpu.roll(mixed, 32, 1)
    mixed = mixed + pltpu.roll(mixed, 64, 1)
    mixed = jnp.concatenate([mixed, mixed], axis=0)
    square = (NC, NC)
    mixed = jnp.where(row_iota(square) // 32 == lane_iota(square) // 32, mixed, 0.0)
    lines = dot3((inv_hi_ref[...], inv_lo_ref[...]), split(mixed), NN)
    upper = row_iota((8, NC)) < 4
    for pair in range(16):
        v = lines[8 * pair : 8 * pair + 8]
        turned = pltpu.roll(v, 4, 0)
        for odd, value in enumerate((jnp.where(upper, v, turned), jnp.where(upper, turned, v))):
            for copy in range(4):
                at = (2 * pair + odd) * 32 + 8 * copy
                out_ref[at : at + 8, :] = value


def point_kernel(mix_ref, bias_ref, hi_ref, lo_ref, out_ref, block_ref):
    block_ref[...] = jnp.zeros((BX, BX), f32)
    for g in range(8):
        block_ref[CH * g : CH * g + CH, CH * g : CH * g + CH] = mix_ref[...]
    point = split(jnp.transpose(block_ref[...]))
    bias = jnp.concatenate([bias_ref[...]] * 8, axis=0)
    bias = jnp.concatenate([bias, bias], axis=1)

    def chunk(i, carry):
        cols = pl.ds(pl.multiple_of(i * 256, 256), 256)
        out_ref[:, cols] = dot3(point, (hi_ref[:, cols], lo_ref[:, cols]), NN) + bias
        return carry

    lax.fori_loop(0, 8, chunk, 0)


def field_kernel(
    in_ref,
    base_ref,
    target_ref,
    proj_ref,
    table_hbm,
    prediction_ref,
    out_ref,
    v_ref,
    before_ref,
    hi_ref,
    lo_ref,
    table_ref,
    sem,
):
    copies = []
    for i in range(8):
        cols = pl.ds(256 * i, 256)
        copies.append(
            pltpu.make_async_copy(table_hbm.at[:, cols], table_ref.at[:, cols], sem.at[i])
        )
        copies[i].start()
    sub = lax.axis_index("sub")
    sign = jnp.where(row_iota((8, NC)) % 2 == 0, -1.0, 1.0).astype(f32)
    keep = row_iota((8, NC)) % 4 < 2
    for j in range(64):
        cos, sin = phase(sub, j // 2)
        first = in_ref[16 * j : 16 * j + 8, :]
        second = in_ref[16 * j + 8 : 16 * j + 16, :]
        low = jnp.where(keep, first, pltpu.roll(second, 2, 0))
        high = jnp.where(keep, pltpu.roll(first, 6, 0), second)
        for h, v in enumerate((low, high)):
            v_ref[8 * j : 8 * j + 8, h * NC : (h + 1) * NC] = v * cos + swap_rows(v) * (sign * sin)
    modes = split(jnp.transpose(v_ref[...]))
    rows = 2 * DEVICES

    def spectral(i):
        cols = slice(256 * i, 256 * i + 256)
        copies[i].wait()
        table = (table_ref[:rows, cols], table_ref[rows:, cols])
        before_ref[i % 2] = base_ref[:, cols] + dot3(modes, table, NN)

    def pointwise(i):
        for g in range(8):
            x, b = g // 2, g % 2
            group = slice(32 * g, 32 * g + 32)
            for q in range(2):
                y = 2 * i + q
                v = before_ref[i % 2, group, q * NC : (q + 1) * NC]
                square, t, half = gelu_parts(v)
                predicted = jnp.sum(proj_ref[...] * (v * half), axis=0, keepdims=True)
                prediction_ref[b, x, y : y + 1, :] = predicted
                miss = predicted - target_ref[b, x, y : y + 1, :]
                bend = (0.5 * SQRT_2_PI) + (0.5 * SQRT_2_PI * 0.134145) * square
                slope = half + (v * (1.0 - t * t)) * bend
                hi, lo = split(slope * (proj_ref[...] * miss))
                hi_ref[group, y * NC : (y + 1) * NC] = hi
                lo_ref[group, y * NC : (y + 1) * NC] = lo

    spectral(0)
    for i in range(8):
        if i < 7:
            spectral(i + 1)
        pointwise(i)
    send_modes(hi_ref, lo_ref, table_ref, sub, out_ref)


def grad_kernel(in_ref, modes_ref, fwd_hi_ref, fwd_lo_ref, out_ref):
    modes_out = line_modes(in_ref, fwd_hi_ref, fwd_lo_ref)
    shape = (64, NC)
    sign = jnp.where(row_iota(shape) % 2 == 0, 1.0, -1.0).astype(f32)
    turned = sign * swap_rows(modes_out)
    right = jnp.where(lane_iota(shape) < 32, modes_out, pltpu.roll(turned, 32, 1))
    left = jnp.transpose(modes_ref[...])[0:32]
    left = jnp.concatenate([left] * M, axis=0) * 0.5
    wide = (32 * M, 64)
    own = row_iota(wide) // 32 == (lane_iota(wide) % 32) // 2
    left = jnp.where(own, left, 0.0)
    grads = dot3(split(left), split(right), NN)
    for kx in range(M):
        block = grads[32 * kx : 32 * kx + 32]
        out_ref[kx, 0] = block[:, 0:32]
        out_ref[kx, 1] = pltpu.roll(block, 96, 1)[:, 0:32]


def vmem():
    return pl.BlockSpec(memory_space=pltpu.VMEM)


def hbm():
    return pl.BlockSpec(memory_space=pltpu.HBM)


def params(mib):
    return pltpu.CompilerParams(vmem_limit_bytes=mib * 1024 * 1024)


def exchange(block):
    return lax.all_to_all(
        block.reshape(DEVICES, 4, NC), ("tile", "sub"), split_axis=0, concat_axis=0, tiled=True
    ).reshape(4 * DEVICES, NC)


def swap(block, axis, odd):
    count = lax.axis_size(axis)
    pairs = []
    for i in range(odd, count - 1, 2):
        pairs += [(i, i + 1), (i + 1, i)]
    return lax.ppermute(block, axis, pairs)


def four(block, at, dim):
    return lax.dynamic_slice_in_dim(block, at, 4, dim)


def local(
    initial_heat,
    cond_level,
    cond_table,
    lift_weight,
    lift_bias,
    mix_weight,
    mix_bias,
    proj_weight,
    spectral_weight,
    target_field,
):
    table = jnp.asarray(plane_table())
    fwd_hi, fwd_lo, inv_hi, inv_lo = [jnp.asarray(v) for v in line_tables()]

    with jax.named_scope("halo"):
        sides = jax.ShapeDtypeStruct((2, 4, 32, FN), f32)
        level_sides = jax.ShapeDtypeStruct((2, 4, 32, FN), jnp.int32)
        rows = jax.ShapeDtypeStruct((2, 2, 8, 4, FN), f32)
        heat_b, level_b, ya, yb, heat_a, level_a = pl.pallas_call(
            pack_kernel,
            out_shape=(sides, level_sides, rows, rows, sides, level_sides),
            in_specs=[hbm()] * 2,
            out_specs=(vmem(),) * 6,
            scratch_shapes=[
                pltpu.VMEM((2, 8, 32, FN), f32),
                pltpu.VMEM((2, 8, 32, FN), jnp.int32),
                pltpu.SemaphoreType.DMA((2,)),
            ],
            compiler_params=params(8),
        )(initial_heat, cond_level)
        heat_b = swap(heat_b, "tile", 1)
        level_b = swap(level_b, "tile", 1)
        ya = swap(ya, "sub", 0)
        yb = swap(yb, "sub", 1)
        heat_a = swap(heat_a, "tile", 0)
        level_a = swap(level_a, "tile", 0)
        corners = jax.ShapeDtypeStruct((2, 2, 4, 8, FN), f32)
        corner_b, corner_a = pl.pallas_call(
            corner_kernel,
            out_shape=(corners, corners),
            in_specs=[vmem()] * 2 + [pl.BlockSpec(memory_space=pl.ANY)] * 2,
            out_specs=(vmem(),) * 2,
            compiler_params=params(8),
        )(ya, yb, heat_b, level_b)
        corner_b = swap(corner_b, "tile", 1)
        corner_a = swap(corner_a, "tile", 0)

    lift = jnp.broadcast_to(
        jnp.concatenate([lift_weight, lift_bias[None]], axis=0)[:, :, None], (3, CH, NC)
    )
    bias = jnp.broadcast_to(mix_bias[:, None], (CH, NC))
    proj = jnp.broadcast_to(proj_weight[:, None], (CH, NC))

    lifted = jax.ShapeDtypeStruct((BX, YZ), bf16)
    blocks = jax.ShapeDtypeStruct((4 * DEVICES, NC), f32)
    grid_shape = (2, 16, 40, FN)
    with jax.named_scope("heat"):
        block, lifted_hi, lifted_lo = pl.pallas_call(
            heat_kernel,
            out_shape=(blocks, lifted, lifted),
            in_specs=[hbm()] * 2 + [vmem()] * 9 + [hbm()] * 2,
            out_specs=(vmem(),) * 3,
            scratch_shapes=[pltpu.VMEM((8, 16, NC), f32)] * 2
            + [pltpu.VMEM(grid_shape, f32)] * 9
            + [
                pltpu.VMEM((512, NC), f32),
                pltpu.VMEM((512, FN), f32),
                pltpu.VMEM((2, 8, 32, FN), jnp.int32),
                pltpu.VMEM((4 * DEVICES, YZ), bf16),
                pltpu.SMEM((16,), f32),
                pltpu.SemaphoreType.DMA((5,)),
            ],
            compiler_params=params(30),
        )(
            initial_heat,
            cond_level,
            heat_a,
            level_a,
            heat_b,
            level_b,
            ya,
            yb,
            corner_a,
            corner_b,
            lift,
            cond_table,
            table,
        )
    block = exchange(block)
    with jax.named_scope("mix"):
        modes_in, block = pl.pallas_call(
            mix_kernel,
            out_shape=(jax.ShapeDtypeStruct((64, NC), f32), blocks),
            in_specs=[vmem()] * 6,
            out_specs=(vmem(),) * 2,
            scratch_shapes=[pltpu.VMEM((CH, 64 * M), f32)],
            compiler_params=params(8),
        )(block, spectral_weight.reshape(M, 2, CH, CH), fwd_hi, fwd_lo, inv_hi, inv_lo)
    block = exchange(block)
    with jax.named_scope("point"):
        base = pl.pallas_call(
            point_kernel,
            out_shape=jax.ShapeDtypeStruct((BX, YZ), f32),
            in_specs=[vmem()] * 4,
            out_specs=vmem(),
            scratch_shapes=[pltpu.VMEM((BX, BX), f32)],
            compiler_params=params(8),
            cost_estimate=pl.CostEstimate(
                flops=6 * BX * BX * YZ, bytes_accessed=16 * BX * YZ, transcendentals=0
            ),
        )(mix_weight, bias, lifted_hi, lifted_lo)
    with jax.named_scope("field"):
        prediction, block = pl.pallas_call(
            field_kernel,
            out_shape=(jax.ShapeDtypeStruct(target_field.shape, f32), blocks),
            in_specs=[vmem()] * 4 + [hbm()],
            out_specs=(vmem(),) * 2,
            scratch_shapes=[
                pltpu.VMEM((2 * DEVICES, BX), f32),
                pltpu.VMEM((2, BX, 256), f32),
                pltpu.VMEM((BX, YZ), bf16),
                pltpu.VMEM((BX, YZ), bf16),
                pltpu.VMEM((4 * DEVICES, YZ), bf16),
                pltpu.SemaphoreType.DMA((8,)),
            ],
            compiler_params=params(24),
        )(block, base, target_field, proj, table)
    block = exchange(block)
    with jax.named_scope("grad"):
        spectral_grad = pl.pallas_call(
            grad_kernel,
            out_shape=jax.ShapeDtypeStruct((M, 2, CH, CH), f32),
            in_specs=[vmem()] * 4,
            out_specs=vmem(),
            compiler_params=params(8),
        )(block, modes_in, fwd_hi, fwd_lo)
    return (prediction, spectral_grad.reshape(1, 1, M, 2, CH, CH))


def solution(mesh):
    in_specs = (
        P(None, "tile", "sub", None),
        P(None, "tile", "sub", None),
        P(),
        P(),
        P(),
        P(),
        P(),
        P(),
        P("sub", "tile", None, None, None, None),
        P(None, "tile", "sub", None),
    )
    out_specs = (P(None, "tile", "sub", None), P("sub", "tile", None, None, None, None))
    return jax.shard_map(local, mesh=mesh, in_specs=in_specs, out_specs=out_specs, check_vma=False)
```

```python
import math

import jax
import jax.numpy as jnp
import numpy as np
from jax import lax
from jax.experimental import pallas as pl
from jax.experimental.pallas import tpu as pltpu
from jax.sharding import PartitionSpec as P

f32 = jnp.float32
bf16 = jnp.bfloat16
highest = lax.Precision.HIGHEST

M = 16
NC = 128
FN = 256
STEPS = 4
TILES = 32
SUBS = 8
DEVICES = TILES * SUBS
CH = 32
BX = 256
YZ = 2048
NT = (((1,), (1,)), ((), ()))
NN = (((1,), (0,)), ((), ()))
SQRT_2_PI = math.sqrt(2.0 / math.pi)


def freq(k):
    return np.where(k >= M // 2, k - M, k)


def split_np(table):
    hi = table.astype(jnp.bfloat16)
    lo = (table - hi.astype(np.float64)).astype(jnp.bfloat16)
    return hi, lo


def stacked_np(table):
    return np.concatenate(split_np(table), axis=0)


def plane_table():
    row = np.arange(2 * DEVICES)
    dest = 4 * (row // 8) + np.array([0, 0, 2, 2, 1, 1, 3, 3])[row % 8]
    imag = row % 2
    pair, block = dest // SUBS, dest % SUBS
    ky = freq(pair % M)
    kz = 2 * block + pair // M
    y = np.repeat(np.arange(16), NC)
    z = np.tile(np.arange(NC), 16)
    cycles = (ky[:, None] * y[None] + kz[:, None] * z[None]) % NC
    angle = cycles * (2.0 * math.pi / NC)
    return stacked_np(np.where(imag[:, None] == 1, -np.sin(angle), np.cos(angle)))


def line_tables():
    k = np.arange(M)
    xp, kx, ro = [v.reshape(-1) for v in np.meshgrid(np.arange(2), k, np.arange(2), indexing="ij")]
    t, _, h, ri = [
        v.reshape(-1)
        for v in np.meshgrid(np.arange(TILES), np.arange(2), np.arange(2), np.arange(2), indexing="ij")
    ]
    x = 4 * t[None] + 2 * h[None] + xp[:, None]
    angle = (freq(kx)[:, None] * x % NC) * (2.0 * math.pi / NC)
    sign = np.where(ro == 0, 1.0, -1.0)[:, None]
    fwd = np.where(ro[:, None] == ri[None], np.cos(angle), sign * np.sin(angle)) / NC**3
    t, h, ro = [
        v.reshape(-1) for v in np.meshgrid(np.arange(TILES), np.arange(2), np.arange(2), indexing="ij")
    ]
    xp, _, kx, ri = [
        v.reshape(-1)
        for v in np.meshgrid(np.arange(2), np.arange(2), k, np.arange(2), indexing="ij")
    ]
    x = 4 * t[:, None] + 2 * h[:, None] + xp[None]
    angle = (freq(kx)[None] * x % NC) * (2.0 * math.pi / NC)
    sign = np.where(ro == 0, -1.0, 1.0)[:, None]
    inv = np.where(ro[:, None] == ri[None], np.cos(angle), sign * np.sin(angle))
    return split_np(fwd) + split_np(inv)


def phase(sub, pair):
    turn = int(freq(np.array(pair % M))) * sub

    def cosine(k):
        k = k & 7
        half = math.sqrt(0.5)
        near = jnp.where(k == 0, 1.0, jnp.where((k == 1) | (k == 7), half, 0.0))
        return jnp.where(k == 4, -1.0, jnp.where((k == 3) | (k == 5), -half, near)).astype(f32)

    return cosine(turn), cosine(turn + 6)


def split(value):
    hi = value.astype(bf16)
    return hi, (value - hi.astype(f32)).astype(bf16)


def dot(a, b, dims):
    return lax.dot_general(a, b, dims, preferred_element_type=f32)


def dot3(a, b, dims):
    return dot(a[0], b[0], dims) + (dot(a[1], b[0], dims) + dot(a[0], b[1], dims))


def row_iota(shape):
    return lax.broadcasted_iota(jnp.int32, shape, 0)


def lane_iota(shape):
    return lax.broadcasted_iota(jnp.int32, shape, 1)


def swap_rows(value):
    rows = value.shape[0]
    return jnp.where(
        row_iota(value.shape) % 2 == 0, pltpu.roll(value, rows - 1, 0), pltpu.roll(value, 1, 0)
    )


def gelu_parts(v):
    square = v * v
    t = jnp.tanh(SQRT_2_PI * (v + 0.044715 * (square * v)))
    half = 0.5 + 0.5 * t
    return square, t, half


def lift_rows(g, y, heat_ref, cond_ref, lift_ref):
    heat = heat_ref[g, y : y + 1, :]
    cond = cond_ref[g, y : y + 1, :]
    v = lift_ref[0] * heat + lift_ref[1] * cond + lift_ref[2]
    return v * gelu_parts(v)[2]


def store_lifted(heat_ref, cond_ref, lift_ref, hi_ref, lo_ref):
    def group(g, carry):
        rows = pl.ds(pl.multiple_of(g * CH, CH), CH)
        for y in range(16):
            hi, lo = split(lift_rows(g, y, heat_ref, cond_ref, lift_ref))
            hi_ref[rows, y * NC : (y + 1) * NC] = hi
            lo_ref[rows, y * NC : (y + 1) * NC] = lo
        return carry

    lax.fori_loop(0, 8, group, 0, unroll=True)


def send_modes(hi_ref, lo_ref, table_ref, sub, out_ref):
    rows = 2 * DEVICES
    both = dot(table_ref[...], hi_ref[...], NT)
    modes = both[:rows] + (both[rows:] + dot(table_ref[:rows], lo_ref[...], NT))
    sign = jnp.where(row_iota((8, NC)) % 2 == 0, 1.0, -1.0).astype(f32)
    keep = row_iota((8, NC)) % 4 < 2
    for j in range(64):
        cos, sin = phase(sub, j // 2)
        halves = []
        for h in range(2):
            v = modes[8 * j : 8 * j + 8, h * NC : (h + 1) * NC]
            halves.append(v * cos + swap_rows(v) * (sign * sin))
        first, second = halves
        out_ref[16 * j : 16 * j + 8, :] = jnp.where(keep, first, pltpu.roll(second, 2, 0))
        out_ref[16 * j + 8 : 16 * j + 16, :] = jnp.where(keep, pltpu.roll(first, 6, 0), second)


def pack_kernel(heat_ref, level_ref, xb_ref, ya_ref, yb_ref, xa_ref):
    at_a = jnp.where(lax.axis_index("tile") % 2 == 0, 4, 0)
    at_b = 4 - at_a
    even = lax.axis_index("sub") % 2 == 0
    for b in range(2):
        for i in range(4):
            for f, source in enumerate((heat_ref, level_ref)):
                xb_ref[f, b, i] = source[b, at_b + i].astype(f32)
                xa_ref[f, b, i] = source[b, at_a + i].astype(f32)
        for i in range(8):
            for f, source in enumerate((heat_ref, level_ref)):
                top = source[b, i, 28:32].astype(f32)
                low = source[b, i, 0:4].astype(f32)
                ya_ref[f, b, i] = jnp.where(even, top, low)
                yb_ref[f, b, i] = jnp.where(even, low, top)


def corner_kernel(ya_ref, yb_ref, xb_ref, corner_b_ref, corner_a_ref):
    at_a = jnp.where(lax.axis_index("tile") % 2 == 0, 4, 0)
    for f in range(2):
        for b in range(2):
            for i in range(4):
                for at, target in ((at_a, corner_a_ref), (4 - at_a, corner_b_ref)):
                    target[f, b, i, 0:4] = ya_ref[f, b, at + i]
                    target[f, b, i, 4:8] = yb_ref[f, b, at + i]


def heat_kernel(
    heat_ref,
    level_ref,
    xa_ref,
    xb_ref,
    ya_ref,
    yb_ref,
    corner_a_ref,
    corner_b_ref,
    lift_ref,
    levels_ref,
    table_ref,
    out_ref,
    hi_ref,
    lo_ref,
    coarse_heat_ref,
    coarse_cond_ref,
    h_ref,
    next_ref,
    c_ref,
    d_ref,
    kx_ref,
    ky_ref,
    kyl_ref,
    kz_ref,
    kzl_ref,
    sum_ref,
    half_ref,
):
    tile = lax.axis_index("tile")
    sub = lax.axis_index("sub")
    even_tile = tile % 2 == 0
    even_sub = sub % 2 == 0
    base_a = jnp.where(even_tile, 12, 0)
    base_b = 12 - base_a
    shape = (40, FN)
    row = row_iota(shape)
    lane = lane_iota(shape)
    last = lane == FN - 1
    first = lane == 0
    top_edge = sub == SUBS - 1
    low_edge = sub == 0
    above = jnp.where(top_edge, 0.0, 1.0).astype(f32)
    below = jnp.where(low_edge, 0.0, 1.0).astype(f32)
    left = jnp.where(tile == 0, 0.0, 1.0).astype(f32)
    right = jnp.where(tile == TILES - 1, 0.0, 1.0).astype(f32)

    def lookup(level):
        bits = [(level & (1 << i)) != 0 for i in range(4)]
        values = [levels_ref[i] for i in range(16)]
        for bit in bits:
            values = [
                jnp.where(bit, values[2 * i + 1], values[2 * i]) for i in range(len(values) // 2)
            ]
        return values[0]

    eight = row_iota((8, FN))
    outer = jnp.where(eight < 4, above, below)

    def outer_layers(i, carry):
        for b in range(2):
            for base, block, corner, side in (
                (base_a, xa_ref, corner_a_ref, jnp.where(even_tile, right, left)),
                (base_b, xb_ref, corner_b_ref, jnp.where(even_tile, left, right)),
            ):
                at = base + i
                h_ref[b, at, 0:32] = block[0, b, i]
                c_ref[b, at, 0:32] = lookup(block[1, b, i].astype(jnp.int32)) * side
                value = corner[0, b, i]
                h_ref[b, at, 32:40] = jnp.where(even_sub, value, pltpu.roll(value, 4, 0))
                value = corner[1, b, i]
                value = jnp.where(even_sub, value, pltpu.roll(value, 4, 0))
                c_ref[b, at, 32:40] = lookup(value.astype(jnp.int32)) * (outer * side)
        return carry

    lax.fori_loop(0, 4, outer_layers, 0)

    def own_layers(i, carry):
        for b in range(2):
            at = 4 + i
            h_ref[b, at, 0:32] = heat_ref[b, i]
            c_ref[b, at, 0:32] = lookup(level_ref[b, i])
            ya = ya_ref[0, b, i]
            yb = yb_ref[0, b, i]
            h_ref[b, at, 32:36] = jnp.where(even_sub, ya, yb)
            h_ref[b, at, 36:40] = jnp.where(even_sub, yb, ya)
            ya = lookup(ya_ref[1, b, i].astype(jnp.int32))
            yb = lookup(yb_ref[1, b, i].astype(jnp.int32))
            c_ref[b, at, 32:36] = jnp.where(even_sub, ya, yb) * above
            c_ref[b, at, 36:40] = jnp.where(even_sub, yb, ya) * below
        return carry

    lax.fori_loop(0, 8, own_layers, 0, unroll=2)

    edge = ((row == 31) & top_edge) | ((row == 39) & low_edge)

    def faces(i, carry):
        for b in range(2):
            c = c_ref[b, i]
            up = pltpu.roll(c, 39, 0)
            down = pltpu.roll(c, 1, 0)
            after = jnp.where(last, 0.0, pltpu.roll(c, FN - 1, 1))
            before = jnp.where(first, 0.0, pltpu.roll(c, 1, 1))
            c_next = c_ref[b, i + 1]
            around = (c_next + c_ref[b, jnp.maximum(i - 1, 0)]) + (up + down) + (after + before)
            d_ref[b, i] = (1.0 - 0.48 * c) - 0.08 * around
            kx_ref[b, i] = 0.08 * (c + c_next)
            ky = jnp.where(edge, 0.0, 0.08 * (c + up))
            ky_ref[b, i] = ky
            kyl_ref[b, i] = pltpu.roll(ky, 1, 0)
            kz_ref[b, i] = jnp.where(last, 0.0, 0.08 * (c + after))
            kzl_ref[b, i] = jnp.where(first, 0.0, 0.08 * (c + before))
        return carry

    lax.fori_loop(0, 15, faces, 0, unroll=3)
    for b in range(2):
        kx_ref[b, 3] = kx_ref[b, 3] * left
        kx_ref[b, 11] = kx_ref[b, 11] * right

    for step in range(1, STEPS + 1):
        source, target = (h_ref, next_ref) if step % 2 == 1 else (next_ref, h_ref)

        def layer_pair(n, carry, source=source, target=target, step=step):
            for j in range(2):
                for b in range(2):
                    i = step + 2 * n + j
                    h = source[b, i]
                    along_x = kx_ref[b, i] * source[b, i + 1] + kx_ref[b, i - 1] * source[b, i - 1]
                    along_y = ky_ref[b, i] * pltpu.roll(h, 39, 0) + kyl_ref[b, i] * pltpu.roll(h, 1, 0)
                    along_z = kz_ref[b, i] * pltpu.roll(h, FN - 1, 1) + kzl_ref[b, i] * pltpu.roll(h, 1, 1)
                    target[b, i] = (d_ref[b, i] * h + along_x) + (along_y + along_z)
            return carry

        lax.fori_loop(0, 8 - step, layer_pair, 0, unroll=True)

    for b in range(2):
        for x in range(4):
            at = 64 * (2 * x + b)
            half_ref[at : at + 32] = h_ref[b, 4 + 2 * x, 0:32] + h_ref[b, 5 + 2 * x, 0:32]
            half_ref[at + 32 : at + 64] = c_ref[b, 4 + 2 * x, 0:32] + c_ref[b, 5 + 2 * x, 0:32]
    pairs = (FN, NC)
    pair = jnp.where(row_iota(pairs) // 2 == lane_iota(pairs), 0.125, 0.0).astype(f32)
    sum_ref[...] = lax.dot_general(
        half_ref[...], pair, NN, precision=highest, preferred_element_type=f32
    )
    for g in range(8):
        for at, target in ((64 * g, coarse_heat_ref), (64 * g + 32, coarse_cond_ref)):
            target[g] = (
                sum_ref[pl.ds(at, 16, stride=2), :] + sum_ref[pl.ds(at + 1, 16, stride=2), :]
            )

    store_lifted(coarse_heat_ref, coarse_cond_ref, lift_ref, hi_ref, lo_ref)
    send_modes(hi_ref, lo_ref, table_ref, sub, out_ref)


def line_modes(in_ref, fwd_hi_ref, fwd_lo_ref):
    sums = []
    for t in range(TILES):
        rows = [in_ref[32 * t + 8 * i : 32 * t + 8 * i + 8, :] for i in range(4)]
        sums.append((rows[0] + rows[1]) + (rows[2] + rows[3]))
    received = split(jnp.concatenate(sums, axis=0))
    both = dot3((fwd_hi_ref[...], fwd_lo_ref[...]), received, NN)
    modes = both[0:32] + pltpu.roll(both[32:64], 64, 1)
    return jnp.concatenate([modes, pltpu.roll(modes, 96, 1)], axis=0)


def mix_kernel(
    in_ref, weight_ref, fwd_hi_ref, fwd_lo_ref, inv_hi_ref, inv_lo_ref, modes_ref, out_ref, w_ref
):
    for kx in range(M):
        for ri in range(2):
            at = kx * 64 + ri * 32
            w_ref[:, at : at + 32] = weight_ref[kx, ri]
    modes = line_modes(in_ref, fwd_hi_ref, fwd_lo_ref)
    modes_ref[...] = modes
    spread = dot3(split(modes[:, 0:32]), split(w_ref[...]), NN)
    shape = (64, NC)
    own = (row_iota(shape) % 32) // 2
    side = lane_iota(shape) // 64
    total = jnp.zeros(shape, f32)
    for part in range(8):
        total = total + jnp.where(own == 2 * part + side, spread[:, part * NC : (part + 1) * NC], 0.0)
    total = total + pltpu.roll(total, 64, 1)
    sign = jnp.where(row_iota(shape) % 2 == 0, -1.0, 1.0).astype(f32)
    mixed = total + sign * swap_rows(pltpu.roll(total, 96, 1))
    mixed = jnp.where(lane_iota(shape) < 32, mixed, 0.0)
    mixed = mixed + pltpu.roll(mixed, 32, 1)
    mixed = mixed + pltpu.roll(mixed, 64, 1)
    mixed = jnp.concatenate([mixed, mixed], axis=0)
    square = (NC, NC)
    mixed = jnp.where(row_iota(square) // 32 == lane_iota(square) // 32, mixed, 0.0)
    lines = dot3((inv_hi_ref[...], inv_lo_ref[...]), split(mixed), NN)
    upper = row_iota((8, NC)) < 4
    for pair in range(16):
        v = lines[8 * pair : 8 * pair + 8]
        turned = pltpu.roll(v, 4, 0)
        for odd, value in enumerate((jnp.where(upper, v, turned), jnp.where(upper, turned, v))):
            for copy in range(4):
                at = (2 * pair + odd) * 32 + 8 * copy
                out_ref[at : at + 8, :] = value


def point_kernel(mix_ref, bias_ref, hi_ref, lo_ref, out_ref, block_ref):
    block_ref[...] = jnp.zeros((BX, BX), f32)
    for g in range(8):
        block_ref[CH * g : CH * g + CH, CH * g : CH * g + CH] = mix_ref[...]
    point = split(jnp.transpose(block_ref[...]))
    bias = jnp.concatenate([bias_ref[...]] * 8, axis=0)
    bias = jnp.concatenate([bias, bias], axis=1)

    def chunk(i, carry):
        cols = pl.ds(pl.multiple_of(i * 256, 256), 256)
        out_ref[:, cols] = dot3(point, (hi_ref[:, cols], lo_ref[:, cols]), NN) + bias
        return carry

    lax.fori_loop(0, 8, chunk, 0)


def field_kernel(
    in_ref,
    base_ref,
    target_ref,
    proj_ref,
    table_hbm,
    prediction_ref,
    out_ref,
    v_ref,
    before_ref,
    hi_ref,
    lo_ref,
    table_ref,
    sem,
):
    copies = []
    for i in range(8):
        cols = pl.ds(256 * i, 256)
        copies.append(
            pltpu.make_async_copy(table_hbm.at[:, cols], table_ref.at[:, cols], sem.at[i])
        )
        copies[i].start()
    sub = lax.axis_index("sub")
    sign = jnp.where(row_iota((8, NC)) % 2 == 0, -1.0, 1.0).astype(f32)
    keep = row_iota((8, NC)) % 4 < 2
    for j in range(64):
        cos, sin = phase(sub, j // 2)
        first = in_ref[16 * j : 16 * j + 8, :]
        second = in_ref[16 * j + 8 : 16 * j + 16, :]
        low = jnp.where(keep, first, pltpu.roll(second, 2, 0))
        high = jnp.where(keep, pltpu.roll(first, 6, 0), second)
        for h, v in enumerate((low, high)):
            v_ref[8 * j : 8 * j + 8, h * NC : (h + 1) * NC] = v * cos + swap_rows(v) * (sign * sin)
    modes = split(jnp.transpose(v_ref[...]))
    rows = 2 * DEVICES

    def spectral(i):
        cols = slice(256 * i, 256 * i + 256)
        copies[i].wait()
        table = (table_ref[:rows, cols], table_ref[rows:, cols])
        before_ref[i % 2] = base_ref[:, cols] + dot3(modes, table, NN)

    def pointwise(i):
        for g in range(8):
            x, b = g // 2, g % 2
            group = slice(32 * g, 32 * g + 32)
            for q in range(2):
                y = 2 * i + q
                v = before_ref[i % 2, group, q * NC : (q + 1) * NC]
                square, t, half = gelu_parts(v)
                predicted = jnp.sum(proj_ref[...] * (v * half), axis=0, keepdims=True)
                prediction_ref[b, x, y : y + 1, :] = predicted
                miss = predicted - target_ref[b, x, y : y + 1, :]
                bend = (0.5 * SQRT_2_PI) + (0.5 * SQRT_2_PI * 0.134145) * square
                slope = half + (v * (1.0 - t * t)) * bend
                hi, lo = split(slope * (proj_ref[...] * miss))
                hi_ref[group, y * NC : (y + 1) * NC] = hi
                lo_ref[group, y * NC : (y + 1) * NC] = lo

    spectral(0)
    for i in range(8):
        if i < 7:
            spectral(i + 1)
        pointwise(i)
    send_modes(hi_ref, lo_ref, table_ref, sub, out_ref)


def grad_kernel(in_ref, modes_ref, fwd_hi_ref, fwd_lo_ref, out_ref):
    modes_out = line_modes(in_ref, fwd_hi_ref, fwd_lo_ref)
    shape = (64, NC)
    sign = jnp.where(row_iota(shape) % 2 == 0, 1.0, -1.0).astype(f32)
    turned = sign * swap_rows(modes_out)
    right = jnp.where(lane_iota(shape) < 32, modes_out, pltpu.roll(turned, 32, 1))
    left = jnp.transpose(modes_ref[...])[0:32]
    left = jnp.concatenate([left] * M, axis=0) * 0.5
    wide = (32 * M, 64)
    own = row_iota(wide) // 32 == (lane_iota(wide) % 32) // 2
    left = jnp.where(own, left, 0.0)
    grads = dot3(split(left), split(right), NN)
    for kx in range(M):
        block = grads[32 * kx : 32 * kx + 32]
        out_ref[kx, 0] = block[:, 0:32]
        out_ref[kx, 1] = pltpu.roll(block, 96, 1)[:, 0:32]


def vmem():
    return pl.BlockSpec(memory_space=pltpu.VMEM)


def smem():
    return pl.BlockSpec(memory_space=pltpu.SMEM)


def cost(giga):
    return pl.CostEstimate(flops=giga * 10**9, bytes_accessed=2**20, transcendentals=0)


def params(mib):
    return pltpu.CompilerParams(vmem_limit_bytes=mib * 1024 * 1024)


def exchange(block):
    return lax.all_to_all(
        block.reshape(DEVICES, 4, NC), ("tile", "sub"), split_axis=0, concat_axis=0, tiled=True
    ).reshape(4 * DEVICES, NC)


def swap(block, axis, odd):
    count = lax.axis_size(axis)
    pairs = []
    for i in range(odd, count - 1, 2):
        pairs += [(i, i + 1), (i + 1, i)]
    return lax.ppermute(block, axis, pairs)


def local(
    initial_heat,
    cond_level,
    cond_table,
    lift_weight,
    lift_bias,
    mix_weight,
    mix_bias,
    proj_weight,
    spectral_weight,
    target_field,
):
    table = jnp.asarray(plane_table())
    fwd_hi, fwd_lo, inv_hi, inv_lo = [jnp.asarray(v) for v in line_tables()]

    with jax.named_scope("halo"):
        sides = jax.ShapeDtypeStruct((2, 2, 4, 32, FN), f32)
        rows = jax.ShapeDtypeStruct((2, 2, 8, 4, FN), f32)
        xb, ya, yb, xa = pl.pallas_call(
            pack_kernel,
            out_shape=(sides, rows, rows, sides),
            in_specs=[vmem()] * 2,
            out_specs=(vmem(),) * 4,
            compiler_params=params(8),
            cost_estimate=cost(8),
        )(initial_heat, cond_level)
        xb = swap(xb, "tile", 1)
        ya = swap(ya, "sub", 0)
        yb = swap(yb, "sub", 1)
        xa = swap(xa, "tile", 0)
        corners = jax.ShapeDtypeStruct((2, 2, 4, 8, FN), f32)
        corner_b, corner_a = pl.pallas_call(
            corner_kernel,
            out_shape=(corners, corners),
            in_specs=[vmem()] * 2 + [pl.BlockSpec(memory_space=pl.ANY)],
            out_specs=(vmem(),) * 2,
            compiler_params=params(8),
            cost_estimate=cost(8),
        )(ya, yb, xb)
        corner_b = swap(corner_b, "tile", 1)
        corner_a = swap(corner_a, "tile", 0)

    lift = jnp.broadcast_to(
        jnp.concatenate([lift_weight, lift_bias[None]], axis=0)[:, :, None], (3, CH, NC)
    )
    bias = jnp.broadcast_to(mix_bias[:, None], (CH, NC))
    proj = jnp.broadcast_to(proj_weight[:, None], (CH, NC))

    lifted = jax.ShapeDtypeStruct((BX, YZ), bf16)
    blocks = jax.ShapeDtypeStruct((4 * DEVICES, NC), f32)
    grid_shape = (2, 16, 40, FN)
    with jax.named_scope("heat"):
        block, lifted_hi, lifted_lo = pl.pallas_call(
            heat_kernel,
            out_shape=(blocks, lifted, lifted),
            in_specs=[vmem()] * 9 + [smem(), vmem()],
            out_specs=(vmem(),) * 3,
            scratch_shapes=[pltpu.VMEM((8, 16, NC), f32)] * 2
            + [pltpu.VMEM(grid_shape, f32)] * 9
            + [
                pltpu.VMEM((512, NC), f32),
                pltpu.VMEM((512, FN), f32),
            ],
            compiler_params=params(24),
            cost_estimate=cost(10),
        )(
            initial_heat,
            cond_level,
            xa,
            xb,
            ya,
            yb,
            corner_a,
            corner_b,
            lift,
            cond_table,
            table,
        )
    block = exchange(block)
    with jax.named_scope("mix"):
        modes_in, block = pl.pallas_call(
            mix_kernel,
            out_shape=(jax.ShapeDtypeStruct((64, NC), f32), blocks),
            in_specs=[vmem()] * 6,
            out_specs=(vmem(),) * 2,
            scratch_shapes=[pltpu.VMEM((CH, 64 * M), f32)],
            compiler_params=params(8),
            cost_estimate=cost(4),
        )(block, spectral_weight.reshape(M, 2, CH, CH), fwd_hi, fwd_lo, inv_hi, inv_lo)
    block = exchange(block)
    with jax.named_scope("point"):
        base = pl.pallas_call(
            point_kernel,
            out_shape=jax.ShapeDtypeStruct((BX, YZ), f32),
            in_specs=[vmem()] * 4,
            out_specs=vmem(),
            scratch_shapes=[pltpu.VMEM((BX, BX), f32)],
            compiler_params=params(8),
            cost_estimate=cost(40),
        )(mix_weight, bias, lifted_hi, lifted_lo)
    with jax.named_scope("field"):
        prediction, block = pl.pallas_call(
            field_kernel,
            out_shape=(jax.ShapeDtypeStruct(target_field.shape, f32), blocks),
            in_specs=[vmem()] * 4 + [pl.BlockSpec(memory_space=pl.ANY)],
            out_specs=(vmem(),) * 2,
            scratch_shapes=[
                pltpu.VMEM((2 * DEVICES, BX), f32),
                pltpu.VMEM((2, BX, 256), f32),
                pltpu.VMEM((BX, YZ), bf16),
                pltpu.VMEM((BX, YZ), bf16),
                pltpu.VMEM((4 * DEVICES, YZ), bf16),
                pltpu.SemaphoreType.DMA((8,)),
            ],
            compiler_params=params(50),
            cost_estimate=cost(6),
        )(block, base, target_field, proj, table)
    block = exchange(block)
    with jax.named_scope("grad"):
        spectral_grad = pl.pallas_call(
            grad_kernel,
            out_shape=jax.ShapeDtypeStruct((M, 2, CH, CH), f32),
            in_specs=[vmem()] * 4,
            out_specs=vmem(),
            compiler_params=params(8),
        )(block, modes_in, fwd_hi, fwd_lo)
    return (prediction, spectral_grad.reshape(1, 1, M, 2, CH, CH))


def solution(mesh):
    in_specs = (
        P(None, "tile", "sub", None),
        P(None, "tile", "sub", None),
        P(),
        P(),
        P(),
        P(),
        P(),
        P(),
        P("sub", "tile", None, None, None, None),
        P(None, "tile", "sub", None),
    )
    out_specs = (P(None, "tile", "sub", None), P("sub", "tile", None, None, None, None))
    return jax.shard_map(local, mesh=mesh, in_specs=in_specs, out_specs=out_specs, check_vma=False)
```

```python
import math

import jax
import jax.numpy as jnp
import numpy as np
from jax import lax
from jax.experimental import pallas as pl
from jax.experimental.pallas import tpu as pltpu
from jax.sharding import PartitionSpec as P

f32 = jnp.float32
bf16 = jnp.bfloat16
highest = lax.Precision.HIGHEST

M = 16
NC = 128
FN = 256
STEPS = 4
TILES = 32
SUBS = 8
DEVICES = TILES * SUBS
CH = 32
BX = 256
YZ = 2048
NT = (((1,), (1,)), ((), ()))
NN = (((1,), (0,)), ((), ()))
SQRT_2_PI = math.sqrt(2.0 / math.pi)


def freq(k):
    return np.where(k >= M // 2, k - M, k)


def split_np(table):
    hi = table.astype(jnp.bfloat16)
    lo = (table - hi.astype(np.float64)).astype(jnp.bfloat16)
    return hi, lo


def stacked_np(table):
    return np.concatenate(split_np(table), axis=0)


def plane_table():
    row = np.arange(2 * DEVICES)
    dest = 4 * (row // 8) + np.array([0, 0, 2, 2, 1, 1, 3, 3])[row % 8]
    imag = row % 2
    pair, block = dest // SUBS, dest % SUBS
    ky = freq(pair % M)
    kz = 2 * block + pair // M
    y = np.repeat(np.arange(16), NC)
    z = np.tile(np.arange(NC), 16)
    cycles = (ky[:, None] * y[None] + kz[:, None] * z[None]) % NC
    angle = cycles * (2.0 * math.pi / NC)
    table = stacked_np(np.where(imag[:, None] == 1, -np.sin(angle), np.cos(angle)))
    return np.ascontiguousarray(table.reshape(4 * DEVICES, 8, 256).transpose(1, 0, 2))


def line_tables():
    k = np.arange(M)
    xp, kx, ro = [v.reshape(-1) for v in np.meshgrid(np.arange(2), k, np.arange(2), indexing="ij")]
    t, _, h, ri = [
        v.reshape(-1)
        for v in np.meshgrid(np.arange(TILES), np.arange(2), np.arange(2), np.arange(2), indexing="ij")
    ]
    x = 4 * t[None] + 2 * h[None] + xp[:, None]
    angle = (freq(kx)[:, None] * x % NC) * (2.0 * math.pi / NC)
    sign = np.where(ro == 0, 1.0, -1.0)[:, None]
    fwd = np.where(ro[:, None] == ri[None], np.cos(angle), sign * np.sin(angle)) / NC**3
    t, h, ro = [
        v.reshape(-1) for v in np.meshgrid(np.arange(TILES), np.arange(2), np.arange(2), indexing="ij")
    ]
    xp, _, kx, ri = [
        v.reshape(-1)
        for v in np.meshgrid(np.arange(2), np.arange(2), k, np.arange(2), indexing="ij")
    ]
    x = 4 * t[:, None] + 2 * h[:, None] + xp[None]
    angle = (freq(kx)[None] * x % NC) * (2.0 * math.pi / NC)
    sign = np.where(ro == 0, -1.0, 1.0)[:, None]
    inv = np.where(ro[:, None] == ri[None], np.cos(angle), sign * np.sin(angle))
    return split_np(fwd) + split_np(inv)


def phase(sub, pair):
    turn = int(freq(np.array(pair % M))) * sub

    def cosine(k):
        k = k & 7
        half = math.sqrt(0.5)
        near = jnp.where(k == 0, 1.0, jnp.where((k == 1) | (k == 7), half, 0.0))
        return jnp.where(k == 4, -1.0, jnp.where((k == 3) | (k == 5), -half, near)).astype(f32)

    return cosine(turn), cosine(turn + 6)


def split(value):
    hi = value.astype(bf16)
    return hi, (value - hi.astype(f32)).astype(bf16)


def dot(a, b, dims):
    return lax.dot_general(a, b, dims, preferred_element_type=f32)


def dot3(a, b, dims):
    return dot(a[0], b[0], dims) + (dot(a[1], b[0], dims) + dot(a[0], b[1], dims))


def row_iota(shape):
    return lax.broadcasted_iota(jnp.int32, shape, 0)


def lane_iota(shape):
    return lax.broadcasted_iota(jnp.int32, shape, 1)


def swap_rows(value):
    rows = value.shape[0]
    return jnp.where(
        row_iota(value.shape) % 2 == 0, pltpu.roll(value, rows - 1, 0), pltpu.roll(value, 1, 0)
    )


def gelu_parts(v):
    square = v * v
    t = jnp.tanh(SQRT_2_PI * (v + 0.044715 * (square * v)))
    half = 0.5 + 0.5 * t
    return square, t, half


def lift_rows(g, y, heat_ref, cond_ref, lift_ref):
    heat = heat_ref[g, y : y + 1, :]
    cond = cond_ref[g, y : y + 1, :]
    v = lift_ref[0] * heat + lift_ref[1] * cond + lift_ref[2]
    return v * gelu_parts(v)[2]


def store_lifted(heat_ref, cond_ref, lift_ref, hi_ref, lo_ref):
    def group(g, carry):
        rows = pl.ds(pl.multiple_of(g * CH, CH), CH)
        for y in range(16):
            hi, lo = split(lift_rows(g, y, heat_ref, cond_ref, lift_ref))
            hi_ref[rows, y * NC : (y + 1) * NC] = hi
            lo_ref[rows, y * NC : (y + 1) * NC] = lo
        return carry

    lax.fori_loop(0, 8, group, 0, unroll=True)


def send_modes(hi_ref, lo_ref, table_ref, sub, out_ref):
    rows = 2 * DEVICES
    table = jnp.concatenate([table_ref[i] for i in range(8)], axis=1)
    both = dot(table, hi_ref[...], NT)
    modes = both[:rows] + (both[rows:] + dot(table[:rows], lo_ref[...], NT))
    sign = jnp.where(row_iota((8, NC)) % 2 == 0, 1.0, -1.0).astype(f32)
    keep = row_iota((8, NC)) % 4 < 2
    for j in range(64):
        cos, sin = phase(sub, j // 2)
        halves = []
        for h in range(2):
            v = modes[8 * j : 8 * j + 8, h * NC : (h + 1) * NC]
            halves.append(v * cos + swap_rows(v) * (sign * sin))
        first, second = halves
        out_ref[16 * j : 16 * j + 8, :] = jnp.where(keep, first, pltpu.roll(second, 2, 0))
        out_ref[16 * j + 8 : 16 * j + 16, :] = jnp.where(keep, pltpu.roll(first, 6, 0), second)


def pack_kernel(
    heat_hbm, level_hbm, xb_ref, ya_ref, yb_ref, xa_ref, heat_ref, level_ref, sem
):
    copies = [
        pltpu.make_async_copy(heat_hbm, heat_ref, sem.at[0]),
        pltpu.make_async_copy(level_hbm, level_ref, sem.at[1]),
    ]
    for copy in copies:
        copy.start()
    for copy in copies:
        copy.wait()
    at_a = jnp.where(lax.axis_index("tile") % 2 == 0, 4, 0)
    at_b = 4 - at_a
    even = lax.axis_index("sub") % 2 == 0
    for b in range(2):
        for i in range(4):
            for f, source in enumerate((heat_ref, level_ref)):
                xb_ref[f, b, i] = source[b, at_b + i].astype(f32)
                xa_ref[f, b, i] = source[b, at_a + i].astype(f32)
        for i in range(8):
            for f, source in enumerate((heat_ref, level_ref)):
                top = source[b, i, 28:32].astype(f32)
                low = source[b, i, 0:4].astype(f32)
                ya_ref[f, b, i] = jnp.where(even, top, low)
                yb_ref[f, b, i] = jnp.where(even, low, top)


def corner_kernel(ya_ref, yb_ref, xb_ref, corner_b_ref, corner_a_ref):
    at_a = jnp.where(lax.axis_index("tile") % 2 == 0, 4, 0)
    for f in range(2):
        for b in range(2):
            for i in range(4):
                for at, target in ((at_a, corner_a_ref), (4 - at_a, corner_b_ref)):
                    target[f, b, i, 0:4] = ya_ref[f, b, at + i]
                    target[f, b, i, 4:8] = yb_ref[f, b, at + i]


def heat_kernel(
    heat_ref,
    level_ref,
    xa_ref,
    xb_ref,
    ya_ref,
    yb_ref,
    corner_a_ref,
    corner_b_ref,
    lift_ref,
    levels_ref,
    table_ref,
    out_ref,
    hi_ref,
    lo_ref,
    coarse_heat_ref,
    coarse_cond_ref,
    h_ref,
    next_ref,
    c_ref,
    d_ref,
    kx_ref,
    ky_ref,
    kyl_ref,
    kz_ref,
    kzl_ref,
    sum_ref,
    half_ref,
):
    tile = lax.axis_index("tile")
    sub = lax.axis_index("sub")
    even_tile = tile % 2 == 0
    even_sub = sub % 2 == 0
    base_a = jnp.where(even_tile, 12, 0)
    base_b = 12 - base_a
    shape = (40, FN)
    row = row_iota(shape)
    lane = lane_iota(shape)
    last = lane == FN - 1
    first = lane == 0
    top_edge = sub == SUBS - 1
    low_edge = sub == 0
    above = jnp.where(top_edge, 0.0, 1.0).astype(f32)
    below = jnp.where(low_edge, 0.0, 1.0).astype(f32)
    left = jnp.where(tile == 0, 0.0, 1.0).astype(f32)
    right = jnp.where(tile == TILES - 1, 0.0, 1.0).astype(f32)

    def lookup(level):
        bits = [(level & (1 << i)) != 0 for i in range(4)]
        values = [levels_ref[i] for i in range(16)]
        for bit in bits:
            values = [
                jnp.where(bit, values[2 * i + 1], values[2 * i]) for i in range(len(values) // 2)
            ]
        return values[0]

    eight = row_iota((8, FN))
    outer = jnp.where(eight < 4, above, below)

    def outer_layers(i, carry):
        for b in range(2):
            for base, block, corner, side in (
                (base_a, xa_ref, corner_a_ref, jnp.where(even_tile, right, left)),
                (base_b, xb_ref, corner_b_ref, jnp.where(even_tile, left, right)),
            ):
                at = base + i
                h_ref[b, at, 0:32] = block[0, b, i]
                c_ref[b, at, 0:32] = lookup(block[1, b, i].astype(jnp.int32)) * side
                value = corner[0, b, i]
                h_ref[b, at, 32:40] = jnp.where(even_sub, value, pltpu.roll(value, 4, 0))
                value = corner[1, b, i]
                value = jnp.where(even_sub, value, pltpu.roll(value, 4, 0))
                c_ref[b, at, 32:40] = lookup(value.astype(jnp.int32)) * (outer * side)
        return carry

    lax.fori_loop(0, 4, outer_layers, 0)

    def own_layers(i, carry):
        for b in range(2):
            at = 4 + i
            h_ref[b, at, 0:32] = heat_ref[b, i]
            c_ref[b, at, 0:32] = lookup(level_ref[b, i])
            ya = ya_ref[0, b, i]
            yb = yb_ref[0, b, i]
            h_ref[b, at, 32:36] = jnp.where(even_sub, ya, yb)
            h_ref[b, at, 36:40] = jnp.where(even_sub, yb, ya)
            ya = lookup(ya_ref[1, b, i].astype(jnp.int32))
            yb = lookup(yb_ref[1, b, i].astype(jnp.int32))
            c_ref[b, at, 32:36] = jnp.where(even_sub, ya, yb) * above
            c_ref[b, at, 36:40] = jnp.where(even_sub, yb, ya) * below
        return carry

    lax.fori_loop(0, 8, own_layers, 0, unroll=2)

    edge = ((row == 31) & top_edge) | ((row == 39) & low_edge)

    def faces(i, carry):
        for b in range(2):
            c = c_ref[b, i]
            up = pltpu.roll(c, 39, 0)
            down = pltpu.roll(c, 1, 0)
            after = jnp.where(last, 0.0, pltpu.roll(c, FN - 1, 1))
            before = jnp.where(first, 0.0, pltpu.roll(c, 1, 1))
            c_next = c_ref[b, i + 1]
            around = (c_next + c_ref[b, jnp.maximum(i - 1, 0)]) + (up + down) + (after + before)
            d_ref[b, i] = (1.0 - 0.48 * c) - 0.08 * around
            kx_ref[b, i] = 0.08 * (c + c_next)
            ky = jnp.where(edge, 0.0, 0.08 * (c + up))
            ky_ref[b, i] = ky
            kyl_ref[b, i] = pltpu.roll(ky, 1, 0)
            kz_ref[b, i] = jnp.where(last, 0.0, 0.08 * (c + after))
            kzl_ref[b, i] = jnp.where(first, 0.0, 0.08 * (c + before))
        return carry

    lax.fori_loop(0, 15, faces, 0, unroll=3)
    for b in range(2):
        kx_ref[b, 3] = kx_ref[b, 3] * left
        kx_ref[b, 11] = kx_ref[b, 11] * right

    for step in range(1, STEPS + 1):
        source, target = (h_ref, next_ref) if step % 2 == 1 else (next_ref, h_ref)

        def layer_pair(n, carry, source=source, target=target, step=step):
            for j in range(2):
                for b in range(2):
                    i = step + 2 * n + j
                    h = source[b, i]
                    along_x = kx_ref[b, i] * source[b, i + 1] + kx_ref[b, i - 1] * source[b, i - 1]
                    along_y = ky_ref[b, i] * pltpu.roll(h, 39, 0) + kyl_ref[b, i] * pltpu.roll(h, 1, 0)
                    along_z = kz_ref[b, i] * pltpu.roll(h, FN - 1, 1) + kzl_ref[b, i] * pltpu.roll(h, 1, 1)
                    target[b, i] = (d_ref[b, i] * h + along_x) + (along_y + along_z)
            return carry

        lax.fori_loop(0, 8 - step, layer_pair, 0, unroll=True)

    for b in range(2):
        for x in range(4):
            at = 64 * (2 * x + b)
            half_ref[at : at + 32] = h_ref[b, 4 + 2 * x, 0:32] + h_ref[b, 5 + 2 * x, 0:32]
            half_ref[at + 32 : at + 64] = c_ref[b, 4 + 2 * x, 0:32] + c_ref[b, 5 + 2 * x, 0:32]
    pairs = (FN, NC)
    pair = jnp.where(row_iota(pairs) // 2 == lane_iota(pairs), 0.125, 0.0).astype(f32)
    sum_ref[...] = lax.dot_general(
        half_ref[...], pair, NN, precision=highest, preferred_element_type=f32
    )
    for g in range(8):
        for at, target in ((64 * g, coarse_heat_ref), (64 * g + 32, coarse_cond_ref)):
            target[g] = (
                sum_ref[pl.ds(at, 16, stride=2), :] + sum_ref[pl.ds(at + 1, 16, stride=2), :]
            )

    store_lifted(coarse_heat_ref, coarse_cond_ref, lift_ref, hi_ref, lo_ref)
    send_modes(hi_ref, lo_ref, table_ref, sub, out_ref)


def line_modes(in_ref, fwd_hi_ref, fwd_lo_ref):
    sums = []
    for t in range(TILES):
        rows = [in_ref[32 * t + 8 * i : 32 * t + 8 * i + 8, :] for i in range(4)]
        sums.append((rows[0] + rows[1]) + (rows[2] + rows[3]))
    received = split(jnp.concatenate(sums, axis=0))
    both = dot3((fwd_hi_ref[...], fwd_lo_ref[...]), received, NN)
    modes = both[0:32] + pltpu.roll(both[32:64], 64, 1)
    return jnp.concatenate([modes, pltpu.roll(modes, 96, 1)], axis=0)


def mix_kernel(
    in_ref, weight_ref, fwd_hi_ref, fwd_lo_ref, inv_hi_ref, inv_lo_ref, modes_ref, out_ref, w_ref
):
    for kx in range(M):
        for ri in range(2):
            at = kx * 64 + ri * 32
            w_ref[:, at : at + 32] = weight_ref[kx, ri]
    modes = line_modes(in_ref, fwd_hi_ref, fwd_lo_ref)
    modes_ref[...] = modes
    spread = dot3(split(modes[:, 0:32]), split(w_ref[...]), NN)
    shape = (64, NC)
    own = (row_iota(shape) % 32) // 2
    side = lane_iota(shape) // 64
    total = jnp.zeros(shape, f32)
    for part in range(8):
        total = total + jnp.where(own == 2 * part + side, spread[:, part * NC : (part + 1) * NC], 0.0)
    total = total + pltpu.roll(total, 64, 1)
    sign = jnp.where(row_iota(shape) % 2 == 0, -1.0, 1.0).astype(f32)
    mixed = total + sign * swap_rows(pltpu.roll(total, 96, 1))
    mixed = jnp.where(lane_iota(shape) < 32, mixed, 0.0)
    mixed = mixed + pltpu.roll(mixed, 32, 1)
    mixed = mixed + pltpu.roll(mixed, 64, 1)
    mixed = jnp.concatenate([mixed, mixed], axis=0)
    square = (NC, NC)
    mixed = jnp.where(row_iota(square) // 32 == lane_iota(square) // 32, mixed, 0.0)
    lines = dot3((inv_hi_ref[...], inv_lo_ref[...]), split(mixed), NN)
    upper = row_iota((8, NC)) < 4
    for pair in range(16):
        v = lines[8 * pair : 8 * pair + 8]
        turned = pltpu.roll(v, 4, 0)
        for odd, value in enumerate((jnp.where(upper, v, turned), jnp.where(upper, turned, v))):
            for copy in range(4):
                at = (2 * pair + odd) * 32 + 8 * copy
                out_ref[at : at + 8, :] = value


def point_kernel(mix_ref, bias_ref, hi_ref, lo_ref, out_ref, block_ref):
    block_ref[...] = jnp.zeros((BX, BX), f32)
    for g in range(8):
        block_ref[CH * g : CH * g + CH, CH * g : CH * g + CH] = mix_ref[...]
    point = split(jnp.transpose(block_ref[...]))
    bias = jnp.concatenate([bias_ref[...]] * 8, axis=0)
    bias = jnp.concatenate([bias, bias], axis=1)

    def chunk(i, carry):
        cols = pl.ds(pl.multiple_of(i * 256, 256), 256)
        out_ref[:, cols] = dot3(point, (hi_ref[:, cols], lo_ref[:, cols]), NN) + bias
        return carry

    lax.fori_loop(0, 8, chunk, 0)


def field_kernel(
    in_ref,
    base_ref,
    target_ref,
    proj_ref,
    table_hbm,
    prediction_ref,
    out_ref,
    v_ref,
    before_ref,
    hi_ref,
    lo_ref,
    table_ref,
    sem,
):
    copies = [
        pltpu.make_async_copy(table_hbm.at[i], table_ref.at[i], sem.at[i]) for i in range(8)
    ]
    for copy in copies:
        copy.start()
    sub = lax.axis_index("sub")
    sign = jnp.where(row_iota((8, NC)) % 2 == 0, -1.0, 1.0).astype(f32)
    keep = row_iota((8, NC)) % 4 < 2
    for j in range(64):
        cos, sin = phase(sub, j // 2)
        first = in_ref[16 * j : 16 * j + 8, :]
        second = in_ref[16 * j + 8 : 16 * j + 16, :]
        low = jnp.where(keep, first, pltpu.roll(second, 2, 0))
        high = jnp.where(keep, pltpu.roll(first, 6, 0), second)
        for h, v in enumerate((low, high)):
            v_ref[8 * j : 8 * j + 8, h * NC : (h + 1) * NC] = v * cos + swap_rows(v) * (sign * sin)
    modes = split(jnp.transpose(v_ref[...]))
    rows = 2 * DEVICES

    def spectral(i):
        cols = slice(256 * i, 256 * i + 256)
        table = (table_ref[i, :rows], table_ref[i, rows:])
        before_ref[i % 2] = base_ref[:, cols] + dot3(modes, table, NN)

    def pointwise(i):
        for g in range(8):
            x, b = g // 2, g % 2
            group = slice(32 * g, 32 * g + 32)
            for q in range(2):
                y = 2 * i + q
                v = before_ref[i % 2, group, q * NC : (q + 1) * NC]
                square, t, half = gelu_parts(v)
                predicted = jnp.sum(proj_ref[...] * (v * half), axis=0, keepdims=True)
                prediction_ref[b, x, y : y + 1, :] = predicted
                miss = predicted - target_ref[b, x, y : y + 1, :]
                bend = (0.5 * SQRT_2_PI) + (0.5 * SQRT_2_PI * 0.134145) * square
                slope = half + (v * (1.0 - t * t)) * bend
                hi, lo = split(slope * (proj_ref[...] * miss))
                hi_ref[group, y * NC : (y + 1) * NC] = hi
                lo_ref[group, y * NC : (y + 1) * NC] = lo

    for copy in copies[:2]:
        copy.wait()
    spectral(0)
    for i in range(8):
        if i == 1:
            for copy in copies[2:]:
                copy.wait()
        if i < 7:
            spectral(i + 1)
        pointwise(i)
    send_modes(hi_ref, lo_ref, table_ref, sub, out_ref)


def grad_kernel(in_ref, modes_ref, fwd_hi_ref, fwd_lo_ref, out_ref):
    modes_out = line_modes(in_ref, fwd_hi_ref, fwd_lo_ref)
    shape = (64, NC)
    sign = jnp.where(row_iota(shape) % 2 == 0, 1.0, -1.0).astype(f32)
    turned = sign * swap_rows(modes_out)
    right = jnp.where(lane_iota(shape) < 32, modes_out, pltpu.roll(turned, 32, 1))
    left = jnp.transpose(modes_ref[...])[0:32]
    left = jnp.concatenate([left] * M, axis=0) * 0.5
    wide = (32 * M, 64)
    own = row_iota(wide) // 32 == (lane_iota(wide) % 32) // 2
    left = jnp.where(own, left, 0.0)
    grads = dot3(split(left), split(right), NN)
    for kx in range(M):
        block = grads[32 * kx : 32 * kx + 32]
        out_ref[kx, 0] = block[:, 0:32]
        out_ref[kx, 1] = pltpu.roll(block, 96, 1)[:, 0:32]


def vmem():
    return pl.BlockSpec(memory_space=pltpu.VMEM)


def smem():
    return pl.BlockSpec(memory_space=pltpu.SMEM)


def cost(giga):
    return pl.CostEstimate(flops=giga * 10**9, bytes_accessed=2**20, transcendentals=0)


def params(mib):
    return pltpu.CompilerParams(vmem_limit_bytes=int(mib * 1024 * 1024))


def exchange(block):
    return lax.all_to_all(
        block.reshape(DEVICES, 4, NC), ("tile", "sub"), split_axis=0, concat_axis=0, tiled=True
    ).reshape(4 * DEVICES, NC)


def swap(block, axis, odd):
    count = lax.axis_size(axis)
    pairs = []
    for i in range(odd, count - 1, 2):
        pairs += [(i, i + 1), (i + 1, i)]
    return lax.ppermute(block, axis, pairs)


def local(
    initial_heat,
    cond_level,
    cond_table,
    lift_weight,
    lift_bias,
    mix_weight,
    mix_bias,
    proj_weight,
    spectral_weight,
    target_field,
):
    table = jnp.asarray(plane_table())
    fwd_hi, fwd_lo, inv_hi, inv_lo = [jnp.asarray(v) for v in line_tables()]

    with jax.named_scope("halo"):
        sides = jax.ShapeDtypeStruct((2, 2, 4, 32, FN), f32)
        rows = jax.ShapeDtypeStruct((2, 2, 8, 4, FN), f32)
        xb, ya, yb, xa = pl.pallas_call(
            pack_kernel,
            out_shape=(sides, rows, rows, sides),
            in_specs=[pl.BlockSpec(memory_space=pl.ANY)] * 2,
            out_specs=(vmem(),) * 4,
            scratch_shapes=[
                pltpu.VMEM((2, 8, 32, FN), f32),
                pltpu.VMEM((2, 8, 32, FN), jnp.int32),
                pltpu.SemaphoreType.DMA((2,)),
            ],
            compiler_params=params(52.5),
            cost_estimate=cost(8),
        )(initial_heat, cond_level)
        xb = swap(xb, "tile", 1)
        ya = swap(ya, "sub", 0)
        yb = swap(yb, "sub", 1)
        xa = swap(xa, "tile", 0)
        corners = jax.ShapeDtypeStruct((2, 2, 4, 8, FN), f32)
        corner_b, corner_a = pl.pallas_call(
            corner_kernel,
            out_shape=(corners, corners),
            in_specs=[vmem()] * 2 + [pl.BlockSpec(memory_space=pl.ANY)],
            out_specs=(vmem(),) * 2,
            compiler_params=params(8),
            cost_estimate=cost(8),
        )(ya, yb, xb)
        corner_b = swap(corner_b, "tile", 1)
        corner_a = swap(corner_a, "tile", 0)

    lift = jnp.broadcast_to(
        jnp.concatenate([lift_weight, lift_bias[None]], axis=0)[:, :, None], (3, CH, NC)
    )
    bias = jnp.broadcast_to(mix_bias[:, None], (CH, NC))
    proj = jnp.broadcast_to(proj_weight[:, None], (CH, NC))

    lifted = jax.ShapeDtypeStruct((BX, YZ), bf16)
    blocks = jax.ShapeDtypeStruct((4 * DEVICES, NC), f32)
    grid_shape = (2, 16, 40, FN)
    with jax.named_scope("heat"):
        block, lifted_hi, lifted_lo = pl.pallas_call(
            heat_kernel,
            out_shape=(blocks, lifted, lifted),
            in_specs=[vmem()] * 9 + [smem(), vmem()],
            out_specs=(vmem(),) * 3,
            scratch_shapes=[pltpu.VMEM((8, 16, NC), f32)] * 2
            + [pltpu.VMEM(grid_shape, f32)] * 9
            + [
                pltpu.VMEM((512, NC), f32),
                pltpu.VMEM((512, FN), f32),
            ],
            compiler_params=params(24),
            cost_estimate=cost(10),
        )(
            initial_heat,
            cond_level,
            xa,
            xb,
            ya,
            yb,
            corner_a,
            corner_b,
            lift,
            cond_table,
            table,
        )
    block = exchange(block)
    with jax.named_scope("mix"):
        modes_in, block = pl.pallas_call(
            mix_kernel,
            out_shape=(jax.ShapeDtypeStruct((64, NC), f32), blocks),
            in_specs=[vmem()] * 6,
            out_specs=(vmem(),) * 2,
            scratch_shapes=[pltpu.VMEM((CH, 64 * M), f32)],
            compiler_params=params(8),
            cost_estimate=cost(4),
        )(block, spectral_weight.reshape(M, 2, CH, CH), fwd_hi, fwd_lo, inv_hi, inv_lo)
    block = exchange(block)
    with jax.named_scope("point"):
        base = pl.pallas_call(
            point_kernel,
            out_shape=jax.ShapeDtypeStruct((BX, YZ), f32),
            in_specs=[vmem()] * 4,
            out_specs=vmem(),
            scratch_shapes=[pltpu.VMEM((BX, BX), f32)],
            compiler_params=params(8),
            cost_estimate=cost(40),
        )(mix_weight, bias, lifted_hi, lifted_lo)
    with jax.named_scope("field"):
        prediction, block = pl.pallas_call(
            field_kernel,
            out_shape=(jax.ShapeDtypeStruct(target_field.shape, f32), blocks),
            in_specs=[vmem()] * 4 + [pl.BlockSpec(memory_space=pl.ANY)],
            out_specs=(vmem(),) * 2,
            scratch_shapes=[
                pltpu.VMEM((2 * DEVICES, BX), f32),
                pltpu.VMEM((2, BX, 256), f32),
                pltpu.VMEM((BX, YZ), bf16),
                pltpu.VMEM((BX, YZ), bf16),
                pltpu.VMEM((8, 4 * DEVICES, 256), bf16),
                pltpu.SemaphoreType.DMA((8,)),
            ],
            compiler_params=params(50),
            cost_estimate=cost(6),
        )(block, base, target_field, proj, table)
    block = exchange(block)
    with jax.named_scope("grad"):
        spectral_grad = pl.pallas_call(
            grad_kernel,
            out_shape=jax.ShapeDtypeStruct((M, 2, CH, CH), f32),
            in_specs=[vmem()] * 4,
            out_specs=vmem(),
            compiler_params=params(8),
        )(block, modes_in, fwd_hi, fwd_lo)
    return (prediction, spectral_grad.reshape(1, 1, M, 2, CH, CH))


def solution(mesh):
    in_specs = (
        P(None, "tile", "sub", None),
        P(None, "tile", "sub", None),
        P(),
        P(),
        P(),
        P(),
        P(),
        P(),
        P("sub", "tile", None, None, None, None),
        P(None, "tile", "sub", None),
    )
    out_specs = (P(None, "tile", "sub", None), P("sub", "tile", None, None, None, None))
    return jax.shard_map(local, mesh=mesh, in_specs=in_specs, out_specs=out_specs, check_vma=False)
```

```python
import math

import jax
import jax.numpy as jnp
import numpy as np
from jax import lax
from jax.experimental import pallas as pl
from jax.experimental.pallas import tpu as pltpu
from jax.sharding import PartitionSpec as P

f32 = jnp.float32
bf16 = jnp.bfloat16
highest = lax.Precision.HIGHEST

M = 16
NC = 128
FN = 256
STEPS = 4
TILES = 32
SUBS = 8
DEVICES = TILES * SUBS
CH = 32
BX = 256
YZ = 2048
NT = (((1,), (1,)), ((), ()))
NN = (((1,), (0,)), ((), ()))
SQRT_2_PI = math.sqrt(2.0 / math.pi)


def freq(k):
    return np.where(k >= M // 2, k - M, k)


def split_np(table):
    hi = table.astype(jnp.bfloat16)
    lo = (table - hi.astype(np.float64)).astype(jnp.bfloat16)
    return hi, lo


def stacked_np(table):
    return np.concatenate(split_np(table), axis=0)


def plane_table():
    row = np.arange(2 * DEVICES)
    dest = 4 * (row // 8) + np.array([0, 0, 2, 2, 1, 1, 3, 3])[row % 8]
    imag = row % 2
    pair, block = dest // SUBS, dest % SUBS
    ky = freq(pair % M)
    kz = 2 * block + pair // M
    y = np.repeat(np.arange(16), NC)
    z = np.tile(np.arange(NC), 16)
    cycles = (ky[:, None] * y[None] + kz[:, None] * z[None]) % NC
    angle = cycles * (2.0 * math.pi / NC)
    table = stacked_np(np.where(imag[:, None] == 1, -np.sin(angle), np.cos(angle)))
    return np.ascontiguousarray(table.reshape(4 * DEVICES, 8, 256).transpose(1, 0, 2))


def line_tables():
    k = np.arange(M)
    xp, kx, ro = [v.reshape(-1) for v in np.meshgrid(np.arange(2), k, np.arange(2), indexing="ij")]
    t, _, h, ri = [
        v.reshape(-1)
        for v in np.meshgrid(np.arange(TILES), np.arange(2), np.arange(2), np.arange(2), indexing="ij")
    ]
    x = 4 * t[None] + 2 * h[None] + xp[:, None]
    angle = (freq(kx)[:, None] * x % NC) * (2.0 * math.pi / NC)
    sign = np.where(ro == 0, 1.0, -1.0)[:, None]
    fwd = np.where(ro[:, None] == ri[None], np.cos(angle), sign * np.sin(angle)) / NC**3
    t, h, ro = [
        v.reshape(-1) for v in np.meshgrid(np.arange(TILES), np.arange(2), np.arange(2), indexing="ij")
    ]
    xp, _, kx, ri = [
        v.reshape(-1)
        for v in np.meshgrid(np.arange(2), np.arange(2), k, np.arange(2), indexing="ij")
    ]
    x = 4 * t[:, None] + 2 * h[:, None] + xp[None]
    angle = (freq(kx)[None] * x % NC) * (2.0 * math.pi / NC)
    sign = np.where(ro == 0, -1.0, 1.0)[:, None]
    inv = np.where(ro[:, None] == ri[None], np.cos(angle), sign * np.sin(angle))
    return split_np(fwd) + split_np(inv)


def phase(sub, pair):
    turn = int(freq(np.array(pair % M))) * sub

    def cosine(k):
        k = k & 7
        half = math.sqrt(0.5)
        near = jnp.where(k == 0, 1.0, jnp.where((k == 1) | (k == 7), half, 0.0))
        return jnp.where(k == 4, -1.0, jnp.where((k == 3) | (k == 5), -half, near)).astype(f32)

    return cosine(turn), cosine(turn + 6)


def split(value):
    hi = value.astype(bf16)
    return hi, (value - hi.astype(f32)).astype(bf16)


def dot(a, b, dims):
    return lax.dot_general(a, b, dims, preferred_element_type=f32)


def dot3(a, b, dims):
    return dot(a[0], b[0], dims) + (dot(a[1], b[0], dims) + dot(a[0], b[1], dims))


def row_iota(shape):
    return lax.broadcasted_iota(jnp.int32, shape, 0)


def lane_iota(shape):
    return lax.broadcasted_iota(jnp.int32, shape, 1)


def swap_rows(value):
    rows = value.shape[0]
    return jnp.where(
        row_iota(value.shape) % 2 == 0, pltpu.roll(value, rows - 1, 0), pltpu.roll(value, 1, 0)
    )


def gelu_parts(v):
    square = v * v
    t = jnp.tanh(SQRT_2_PI * (v + 0.044715 * (square * v)))
    half = 0.5 + 0.5 * t
    return square, t, half


def lift_rows(g, y, heat_ref, cond_ref, lift_ref):
    heat = heat_ref[g, y : y + 1, :]
    cond = cond_ref[g, y : y + 1, :]
    v = lift_ref[0] * heat + lift_ref[1] * cond + lift_ref[2]
    return v * gelu_parts(v)[2]


def store_lifted(heat_ref, cond_ref, lift_ref, hi_ref, lo_ref):
    def group(g, carry):
        rows = pl.ds(pl.multiple_of(g * CH, CH), CH)
        for y in range(16):
            hi, lo = split(lift_rows(g, y, heat_ref, cond_ref, lift_ref))
            hi_ref[rows, y * NC : (y + 1) * NC] = hi
            lo_ref[rows, y * NC : (y + 1) * NC] = lo
        return carry

    lax.fori_loop(0, 8, group, 0, unroll=True)


def send_modes(hi_ref, lo_ref, table_ref, sub, out_ref):
    rows = 2 * DEVICES
    table = jnp.concatenate([table_ref[i] for i in range(8)], axis=1)
    both = dot(table, hi_ref[...], NT)
    modes = both[:rows] + (both[rows:] + dot(table[:rows], lo_ref[...], NT))
    sign = jnp.where(row_iota((8, NC)) % 2 == 0, 1.0, -1.0).astype(f32)
    keep = row_iota((8, NC)) % 4 < 2
    for j in range(64):
        cos, sin = phase(sub, j // 2)
        halves = []
        for h in range(2):
            v = modes[8 * j : 8 * j + 8, h * NC : (h + 1) * NC]
            halves.append(v * cos + swap_rows(v) * (sign * sin))
        first, second = halves
        out_ref[16 * j : 16 * j + 8, :] = jnp.where(keep, first, pltpu.roll(second, 2, 0))
        out_ref[16 * j + 8 : 16 * j + 16, :] = jnp.where(keep, pltpu.roll(first, 6, 0), second)


def pack_kernel(
    heat_hbm, level_hbm, xb_ref, ya_ref, yb_ref, xa_ref, heat_ref, level_ref, sem
):
    copies = [
        pltpu.make_async_copy(heat_hbm, heat_ref, sem.at[0]),
        pltpu.make_async_copy(level_hbm, level_ref, sem.at[1]),
    ]
    for copy in copies:
        copy.start()
    for copy in copies:
        copy.wait()
    at_a = jnp.where(lax.axis_index("tile") % 2 == 0, 4, 0)
    at_b = 4 - at_a
    even = lax.axis_index("sub") % 2 == 0
    for b in range(2):
        for i in range(4):
            for f, source in enumerate((heat_ref, level_ref)):
                xb_ref[f, b, i] = source[b, at_b + i].astype(f32)
                xa_ref[f, b, i] = source[b, at_a + i].astype(f32)
        for i in range(8):
            for f, source in enumerate((heat_ref, level_ref)):
                top = source[b, i, 28:32].astype(f32)
                low = source[b, i, 0:4].astype(f32)
                ya_ref[f, b, i] = jnp.where(even, top, low)
                yb_ref[f, b, i] = jnp.where(even, low, top)


def corner_kernel(ya_ref, yb_ref, xb_ref, corner_b_ref, corner_a_ref):
    at_a = jnp.where(lax.axis_index("tile") % 2 == 0, 4, 0)
    for f in range(2):
        for b in range(2):
            for i in range(4):
                for at, target in ((at_a, corner_a_ref), (4 - at_a, corner_b_ref)):
                    target[f, b, i, 0:4] = ya_ref[f, b, at + i]
                    target[f, b, i, 4:8] = yb_ref[f, b, at + i]


def heat_kernel(
    heat_ref,
    level_ref,
    xa_ref,
    xb_ref,
    ya_ref,
    yb_ref,
    corner_a_ref,
    corner_b_ref,
    lift_ref,
    levels_ref,
    table_ref,
    out_ref,
    hi_ref,
    lo_ref,
    coarse_heat_ref,
    coarse_cond_ref,
    h_ref,
    next_ref,
    c_ref,
    d_ref,
    kx_ref,
    ky_ref,
    kyl_ref,
    kz_ref,
    kzl_ref,
    sum_ref,
    half_ref,
):
    tile = lax.axis_index("tile")
    sub = lax.axis_index("sub")
    even_tile = tile % 2 == 0
    even_sub = sub % 2 == 0
    base_a = jnp.where(even_tile, 12, 0)
    base_b = 12 - base_a
    shape = (40, FN)
    row = row_iota(shape)
    lane = lane_iota(shape)
    last = lane == FN - 1
    first = lane == 0
    top_edge = sub == SUBS - 1
    low_edge = sub == 0
    above = jnp.where(top_edge, 0.0, 1.0).astype(f32)
    below = jnp.where(low_edge, 0.0, 1.0).astype(f32)
    left = jnp.where(tile == 0, 0.0, 1.0).astype(f32)
    right = jnp.where(tile == TILES - 1, 0.0, 1.0).astype(f32)

    def lookup(level):
        bits = [(level & (1 << i)) != 0 for i in range(4)]
        values = [levels_ref[i] for i in range(16)]
        for bit in bits:
            values = [
                jnp.where(bit, values[2 * i + 1], values[2 * i]) for i in range(len(values) // 2)
            ]
        return values[0]

    eight = row_iota((8, FN))
    outer = jnp.where(eight < 4, above, below)

    def outer_layers(i, carry):
        for b in range(2):
            for base, block, corner, side in (
                (base_a, xa_ref, corner_a_ref, jnp.where(even_tile, right, left)),
                (base_b, xb_ref, corner_b_ref, jnp.where(even_tile, left, right)),
            ):
                at = base + i
                h_ref[b, at, 0:32] = block[0, b, i]
                c_ref[b, at, 0:32] = lookup(block[1, b, i].astype(jnp.int32)) * side
                value = corner[0, b, i]
                h_ref[b, at, 32:40] = jnp.where(even_sub, value, pltpu.roll(value, 4, 0))
                value = corner[1, b, i]
                value = jnp.where(even_sub, value, pltpu.roll(value, 4, 0))
                c_ref[b, at, 32:40] = lookup(value.astype(jnp.int32)) * (outer * side)
        return carry

    lax.fori_loop(0, 4, outer_layers, 0, unroll=True)

    def own_layers(i, carry):
        for b in range(2):
            at = 4 + i
            h_ref[b, at, 0:32] = heat_ref[b, i]
            c_ref[b, at, 0:32] = lookup(level_ref[b, i])
            ya = ya_ref[0, b, i]
            yb = yb_ref[0, b, i]
            h_ref[b, at, 32:36] = jnp.where(even_sub, ya, yb)
            h_ref[b, at, 36:40] = jnp.where(even_sub, yb, ya)
            ya = lookup(ya_ref[1, b, i].astype(jnp.int32))
            yb = lookup(yb_ref[1, b, i].astype(jnp.int32))
            c_ref[b, at, 32:36] = jnp.where(even_sub, ya, yb) * above
            c_ref[b, at, 36:40] = jnp.where(even_sub, yb, ya) * below
        return carry

    lax.fori_loop(0, 8, own_layers, 0, unroll=2)

    edge = ((row == 31) & top_edge) | ((row == 39) & low_edge)

    def faces(i, carry):
        for b in range(2):
            c = c_ref[b, i]
            up = pltpu.roll(c, 39, 0)
            down = pltpu.roll(c, 1, 0)
            after = jnp.where(last, 0.0, pltpu.roll(c, FN - 1, 1))
            before = jnp.where(first, 0.0, pltpu.roll(c, 1, 1))
            c_next = c_ref[b, i + 1]
            around = (c_next + c_ref[b, jnp.maximum(i - 1, 0)]) + (up + down) + (after + before)
            d_ref[b, i] = (1.0 - 0.48 * c) - 0.08 * around
            kx_ref[b, i] = 0.08 * (c + c_next)
            ky = jnp.where(edge, 0.0, 0.08 * (c + up))
            ky_ref[b, i] = ky
            kyl_ref[b, i] = pltpu.roll(ky, 1, 0)
            kz_ref[b, i] = jnp.where(last, 0.0, 0.08 * (c + after))
            kzl_ref[b, i] = jnp.where(first, 0.0, 0.08 * (c + before))
        return carry

    lax.fori_loop(0, 15, faces, 0, unroll=3)
    for b in range(2):
        kx_ref[b, 3] = kx_ref[b, 3] * left
        kx_ref[b, 11] = kx_ref[b, 11] * right

    for step in range(1, STEPS + 1):
        source, target = (h_ref, next_ref) if step % 2 == 1 else (next_ref, h_ref)

        def layer_pair(n, carry, source=source, target=target, step=step):
            for j in range(2):
                for b in range(2):
                    i = step + 2 * n + j
                    h = source[b, i]
                    along_x = kx_ref[b, i] * source[b, i + 1] + kx_ref[b, i - 1] * source[b, i - 1]
                    along_y = ky_ref[b, i] * pltpu.roll(h, 39, 0) + kyl_ref[b, i] * pltpu.roll(h, 1, 0)
                    along_z = kz_ref[b, i] * pltpu.roll(h, FN - 1, 1) + kzl_ref[b, i] * pltpu.roll(h, 1, 1)
                    target[b, i] = (d_ref[b, i] * h + along_x) + (along_y + along_z)
            return carry

        lax.fori_loop(0, 8 - step, layer_pair, 0, unroll=True)

    for b in range(2):
        for x in range(4):
            at = 64 * (2 * x + b)
            half_ref[at : at + 32] = h_ref[b, 4 + 2 * x, 0:32] + h_ref[b, 5 + 2 * x, 0:32]
            half_ref[at + 32 : at + 64] = c_ref[b, 4 + 2 * x, 0:32] + c_ref[b, 5 + 2 * x, 0:32]
    pairs = (FN, NC)
    pair = jnp.where(row_iota(pairs) // 2 == lane_iota(pairs), 0.125, 0.0).astype(f32)
    sum_ref[...] = lax.dot_general(
        half_ref[...], pair, NN, precision=highest, preferred_element_type=f32
    )
    for g in range(8):
        for at, target in ((64 * g, coarse_heat_ref), (64 * g + 32, coarse_cond_ref)):
            target[g] = (
                sum_ref[pl.ds(at, 16, stride=2), :] + sum_ref[pl.ds(at + 1, 16, stride=2), :]
            )

    store_lifted(coarse_heat_ref, coarse_cond_ref, lift_ref, hi_ref, lo_ref)
    send_modes(hi_ref, lo_ref, table_ref, sub, out_ref)


def line_modes(in_ref, fwd_hi_ref, fwd_lo_ref):
    sums = []
    for t in range(TILES):
        rows = [in_ref[32 * t + 8 * i : 32 * t + 8 * i + 8, :] for i in range(4)]
        sums.append((rows[0] + rows[1]) + (rows[2] + rows[3]))
    received = split(jnp.concatenate(sums, axis=0))
    both = dot3((fwd_hi_ref[...], fwd_lo_ref[...]), received, NN)
    modes = both[0:32] + pltpu.roll(both[32:64], 64, 1)
    return jnp.concatenate([modes, pltpu.roll(modes, 96, 1)], axis=0)


def mix_kernel(
    in_ref, weight_ref, fwd_hi_ref, fwd_lo_ref, inv_hi_ref, inv_lo_ref, modes_ref, out_ref, w_ref
):
    for kx in range(M):
        for ri in range(2):
            at = kx * 64 + ri * 32
            w_ref[:, at : at + 32] = weight_ref[kx, ri]
    modes = line_modes(in_ref, fwd_hi_ref, fwd_lo_ref)
    modes_ref[...] = modes
    spread = dot3(split(modes[:, 0:32]), split(w_ref[...]), NN)
    shape = (64, NC)
    own = (row_iota(shape) % 32) // 2
    side = lane_iota(shape) // 64
    total = jnp.zeros(shape, f32)
    for part in range(8):
        total = total + jnp.where(own == 2 * part + side, spread[:, part * NC : (part + 1) * NC], 0.0)
    total = total + pltpu.roll(total, 64, 1)
    sign = jnp.where(row_iota(shape) % 2 == 0, -1.0, 1.0).astype(f32)
    mixed = total + sign * swap_rows(pltpu.roll(total, 96, 1))
    mixed = jnp.where(lane_iota(shape) < 32, mixed, 0.0)
    mixed = mixed + pltpu.roll(mixed, 32, 1)
    mixed = mixed + pltpu.roll(mixed, 64, 1)
    mixed = jnp.concatenate([mixed, mixed], axis=0)
    square = (NC, NC)
    mixed = jnp.where(row_iota(square) // 32 == lane_iota(square) // 32, mixed, 0.0)
    lines = dot3((inv_hi_ref[...], inv_lo_ref[...]), split(mixed), NN)
    upper = row_iota((8, NC)) < 4
    for pair in range(16):
        v = lines[8 * pair : 8 * pair + 8]
        turned = pltpu.roll(v, 4, 0)
        for odd, value in enumerate((jnp.where(upper, v, turned), jnp.where(upper, turned, v))):
            for copy in range(4):
                at = (2 * pair + odd) * 32 + 8 * copy
                out_ref[at : at + 8, :] = value


def point_kernel(mix_ref, bias_ref, hi_ref, lo_ref, out_ref, block_ref):
    block_ref[...] = jnp.zeros((BX, BX), f32)
    for g in range(8):
        block_ref[CH * g : CH * g + CH, CH * g : CH * g + CH] = mix_ref[...]
    point = split(jnp.transpose(block_ref[...]))
    bias = jnp.concatenate([bias_ref[...]] * 8, axis=0)
    bias = jnp.concatenate([bias, bias], axis=1)

    def chunk(i, carry):
        cols = pl.ds(pl.multiple_of(i * 256, 256), 256)
        out_ref[:, cols] = dot3(point, (hi_ref[:, cols], lo_ref[:, cols]), NN) + bias
        return carry

    lax.fori_loop(0, 8, chunk, 0)


def field_kernel(
    in_ref,
    base_ref,
    target_ref,
    proj_ref,
    table_hbm,
    prediction_ref,
    out_ref,
    v_ref,
    before_ref,
    hi_ref,
    lo_ref,
    table_ref,
    sem,
):
    copies = [
        pltpu.make_async_copy(table_hbm.at[i], table_ref.at[i], sem.at[i]) for i in range(8)
    ]
    for copy in copies:
        copy.start()
    sub = lax.axis_index("sub")
    sign = jnp.where(row_iota((8, NC)) % 2 == 0, -1.0, 1.0).astype(f32)
    keep = row_iota((8, NC)) % 4 < 2
    for j in range(64):
        cos, sin = phase(sub, j // 2)
        first = in_ref[16 * j : 16 * j + 8, :]
        second = in_ref[16 * j + 8 : 16 * j + 16, :]
        low = jnp.where(keep, first, pltpu.roll(second, 2, 0))
        high = jnp.where(keep, pltpu.roll(first, 6, 0), second)
        for h, v in enumerate((low, high)):
            v_ref[8 * j : 8 * j + 8, h * NC : (h + 1) * NC] = v * cos + swap_rows(v) * (sign * sin)
    modes = split(jnp.transpose(v_ref[...]))
    rows = 2 * DEVICES

    def spectral(i):
        cols = slice(256 * i, 256 * i + 256)
        table = (table_ref[i, :rows], table_ref[i, rows:])
        before_ref[i % 2] = base_ref[:, cols] + dot3(modes, table, NN)

    def pointwise(i):
        for g in range(8):
            x, b = g // 2, g % 2
            group = slice(32 * g, 32 * g + 32)
            for q in range(2):
                y = 2 * i + q
                v = before_ref[i % 2, group, q * NC : (q + 1) * NC]
                square, t, half = gelu_parts(v)
                predicted = jnp.sum(proj_ref[...] * (v * half), axis=0, keepdims=True)
                prediction_ref[b, x, y : y + 1, :] = predicted
                miss = predicted - target_ref[b, x, y : y + 1, :]
                bend = (0.5 * SQRT_2_PI) + (0.5 * SQRT_2_PI * 0.134145) * square
                slope = half + (v * (1.0 - t * t)) * bend
                hi, lo = split(slope * (proj_ref[...] * miss))
                hi_ref[group, y * NC : (y + 1) * NC] = hi
                lo_ref[group, y * NC : (y + 1) * NC] = lo

    copies[0].wait()
    spectral(0)
    for i in range(8):
        if i in (0, 2):
            for copy in copies[1:4] if i == 0 else copies[4:]:
                copy.wait()
        if i < 7:
            spectral(i + 1)
        pointwise(i)
    send_modes(hi_ref, lo_ref, table_ref, sub, out_ref)


def grad_kernel(in_ref, modes_ref, fwd_hi_ref, fwd_lo_ref, out_ref):
    modes_out = line_modes(in_ref, fwd_hi_ref, fwd_lo_ref)
    shape = (64, NC)
    sign = jnp.where(row_iota(shape) % 2 == 0, 1.0, -1.0).astype(f32)
    turned = sign * swap_rows(modes_out)
    right = jnp.where(lane_iota(shape) < 32, modes_out, pltpu.roll(turned, 32, 1))
    left = jnp.transpose(modes_ref[...])[0:32]
    left = jnp.concatenate([left] * M, axis=0) * 0.5
    wide = (32 * M, 64)
    own = row_iota(wide) // 32 == (lane_iota(wide) % 32) // 2
    left = jnp.where(own, left, 0.0)
    grads = dot3(split(left), split(right), NN)
    for kx in range(M):
        block = grads[32 * kx : 32 * kx + 32]
        out_ref[kx, 0] = block[:, 0:32]
        out_ref[kx, 1] = pltpu.roll(block, 96, 1)[:, 0:32]


def vmem():
    return pl.BlockSpec(memory_space=pltpu.VMEM)


def smem():
    return pl.BlockSpec(memory_space=pltpu.SMEM)


def cost(giga):
    return pl.CostEstimate(flops=giga * 10**9, bytes_accessed=2**20, transcendentals=0)


def params(mib):
    return pltpu.CompilerParams(vmem_limit_bytes=int(mib * 1024 * 1024))


def exchange(block):
    return lax.all_to_all(
        block.reshape(DEVICES, 4, NC), ("tile", "sub"), split_axis=0, concat_axis=0, tiled=True
    ).reshape(4 * DEVICES, NC)


def swap(block, axis, odd):
    count = lax.axis_size(axis)
    pairs = []
    for i in range(odd, count - 1, 2):
        pairs += [(i, i + 1), (i + 1, i)]
    return lax.ppermute(block, axis, pairs)


def local(
    initial_heat,
    cond_level,
    cond_table,
    lift_weight,
    lift_bias,
    mix_weight,
    mix_bias,
    proj_weight,
    spectral_weight,
    target_field,
):
    table = jnp.asarray(plane_table())
    fwd_hi, fwd_lo, inv_hi, inv_lo = [jnp.asarray(v) for v in line_tables()]

    with jax.named_scope("halo"):
        sides = jax.ShapeDtypeStruct((2, 2, 4, 32, FN), f32)
        rows = jax.ShapeDtypeStruct((2, 2, 8, 4, FN), f32)
        xb, ya, yb, xa = pl.pallas_call(
            pack_kernel,
            out_shape=(sides, rows, rows, sides),
            in_specs=[pl.BlockSpec(memory_space=pl.ANY)] * 2,
            out_specs=(vmem(),) * 4,
            scratch_shapes=[
                pltpu.VMEM((2, 8, 32, FN), f32),
                pltpu.VMEM((2, 8, 32, FN), jnp.int32),
                pltpu.SemaphoreType.DMA((2,)),
            ],
            compiler_params=params(52.5),
            cost_estimate=cost(8),
        )(initial_heat, cond_level)
        xb = swap(xb, "tile", 1)
        ya = swap(ya, "sub", 0)
        yb = swap(yb, "sub", 1)
        xa = swap(xa, "tile", 0)
        corners = jax.ShapeDtypeStruct((2, 2, 4, 8, FN), f32)
        corner_b, corner_a = pl.pallas_call(
            corner_kernel,
            out_shape=(corners, corners),
            in_specs=[vmem()] * 2 + [pl.BlockSpec(memory_space=pl.ANY)],
            out_specs=(vmem(),) * 2,
            compiler_params=params(8),
            cost_estimate=cost(8),
        )(ya, yb, xb)
        corner_b = swap(corner_b, "tile", 1)
        corner_a = swap(corner_a, "tile", 0)

    lift = jnp.broadcast_to(
        jnp.concatenate([lift_weight, lift_bias[None]], axis=0)[:, :, None], (3, CH, NC)
    )
    bias = jnp.broadcast_to(mix_bias[:, None], (CH, NC))
    proj = jnp.broadcast_to(proj_weight[:, None], (CH, NC))

    lifted = jax.ShapeDtypeStruct((BX, YZ), bf16)
    blocks = jax.ShapeDtypeStruct((4 * DEVICES, NC), f32)
    grid_shape = (2, 16, 40, FN)
    with jax.named_scope("heat"):
        block, lifted_hi, lifted_lo = pl.pallas_call(
            heat_kernel,
            out_shape=(blocks, lifted, lifted),
            in_specs=[vmem()] * 9 + [smem(), vmem()],
            out_specs=(vmem(),) * 3,
            scratch_shapes=[pltpu.VMEM((8, 16, NC), f32)] * 2
            + [pltpu.VMEM(grid_shape, f32)] * 9
            + [
                pltpu.VMEM((512, NC), f32),
                pltpu.VMEM((512, FN), f32),
            ],
            compiler_params=params(24),
            cost_estimate=cost(10),
        )(
            initial_heat,
            cond_level,
            xa,
            xb,
            ya,
            yb,
            corner_a,
            corner_b,
            lift,
            cond_table,
            table,
        )
    block = exchange(block)
    with jax.named_scope("mix"):
        modes_in, block = pl.pallas_call(
            mix_kernel,
            out_shape=(jax.ShapeDtypeStruct((64, NC), f32), blocks),
            in_specs=[vmem()] * 6,
            out_specs=(vmem(),) * 2,
            scratch_shapes=[pltpu.VMEM((CH, 64 * M), f32)],
            compiler_params=params(8),
            cost_estimate=cost(4),
        )(block, spectral_weight.reshape(M, 2, CH, CH), fwd_hi, fwd_lo, inv_hi, inv_lo)
    block = exchange(block)
    with jax.named_scope("point"):
        base = pl.pallas_call(
            point_kernel,
            out_shape=jax.ShapeDtypeStruct((BX, YZ), f32),
            in_specs=[vmem()] * 4,
            out_specs=vmem(),
            scratch_shapes=[pltpu.VMEM((BX, BX), f32)],
            compiler_params=params(8),
            cost_estimate=cost(40),
        )(mix_weight, bias, lifted_hi, lifted_lo)
    with jax.named_scope("field"):
        prediction, block = pl.pallas_call(
            field_kernel,
            out_shape=(jax.ShapeDtypeStruct(target_field.shape, f32), blocks),
            in_specs=[vmem()] * 4 + [pl.BlockSpec(memory_space=pl.ANY)],
            out_specs=(vmem(),) * 2,
            scratch_shapes=[
                pltpu.VMEM((2 * DEVICES, BX), f32),
                pltpu.VMEM((2, BX, 256), f32),
                pltpu.VMEM((BX, YZ), bf16),
                pltpu.VMEM((BX, YZ), bf16),
                pltpu.VMEM((8, 4 * DEVICES, 256), bf16),
                pltpu.SemaphoreType.DMA((8,)),
            ],
            compiler_params=params(50),
            cost_estimate=cost(6),
        )(block, base, target_field, proj, table)
    block = exchange(block)
    with jax.named_scope("grad"):
        spectral_grad = pl.pallas_call(
            grad_kernel,
            out_shape=jax.ShapeDtypeStruct((M, 2, CH, CH), f32),
            in_specs=[vmem()] * 4,
            out_specs=vmem(),
            compiler_params=params(8),
        )(block, modes_in, fwd_hi, fwd_lo)
    return (prediction, spectral_grad.reshape(1, 1, M, 2, CH, CH))


def solution(mesh):
    in_specs = (
        P(None, "tile", "sub", None),
        P(None, "tile", "sub", None),
        P(),
        P(),
        P(),
        P(),
        P(),
        P(),
        P("sub", "tile", None, None, None, None),
        P(None, "tile", "sub", None),
    )
    out_specs = (P(None, "tile", "sub", None), P("sub", "tile", None, None, None, None))
    return jax.shard_map(local, mesh=mesh, in_specs=in_specs, out_specs=out_specs, check_vma=False)
```

```python
import math

import jax
import jax.numpy as jnp
import numpy as np
from jax import lax
from jax.experimental import pallas as pl
from jax.experimental.pallas import tpu as pltpu
from jax.sharding import PartitionSpec as P

f32 = jnp.float32
bf16 = jnp.bfloat16
highest = lax.Precision.HIGHEST

M = 16
NC = 128
FN = 256
STEPS = 4
TILES = 32
SUBS = 8
DEVICES = TILES * SUBS
CH = 32
BX = 256
YZ = 2048
NT = (((1,), (1,)), ((), ()))
NN = (((1,), (0,)), ((), ()))
SQRT_2_PI = math.sqrt(2.0 / math.pi)


def freq(k):
    return np.where(k >= M // 2, k - M, k)


def split_np(table):
    hi = table.astype(jnp.bfloat16)
    lo = (table - hi.astype(np.float64)).astype(jnp.bfloat16)
    return hi, lo


def stacked_np(table):
    return np.concatenate(split_np(table), axis=0)


def plane_table():
    row = np.arange(2 * DEVICES)
    dest = 4 * (row // 8) + np.array([0, 0, 2, 2, 1, 1, 3, 3])[row % 8]
    imag = row % 2
    pair, block = dest // SUBS, dest % SUBS
    ky = freq(pair % M)
    kz = 2 * block + pair // M
    y = np.repeat(np.arange(16), NC)
    z = np.tile(np.arange(NC), 16)
    cycles = (ky[:, None] * y[None] + kz[:, None] * z[None]) % NC
    angle = cycles * (2.0 * math.pi / NC)
    table = stacked_np(np.where(imag[:, None] == 1, -np.sin(angle), np.cos(angle)))
    return np.ascontiguousarray(table.reshape(4 * DEVICES, 8, 256).transpose(1, 0, 2))


def line_tables():
    k = np.arange(M)
    xp, kx, ro = [v.reshape(-1) for v in np.meshgrid(np.arange(2), k, np.arange(2), indexing="ij")]
    t, _, h, ri = [
        v.reshape(-1)
        for v in np.meshgrid(np.arange(TILES), np.arange(2), np.arange(2), np.arange(2), indexing="ij")
    ]
    x = 4 * t[None] + 2 * h[None] + xp[:, None]
    angle = (freq(kx)[:, None] * x % NC) * (2.0 * math.pi / NC)
    sign = np.where(ro == 0, 1.0, -1.0)[:, None]
    fwd = np.where(ro[:, None] == ri[None], np.cos(angle), sign * np.sin(angle)) / NC**3
    t, h, ro = [
        v.reshape(-1) for v in np.meshgrid(np.arange(TILES), np.arange(2), np.arange(2), indexing="ij")
    ]
    xp, _, kx, ri = [
        v.reshape(-1)
        for v in np.meshgrid(np.arange(2), np.arange(2), k, np.arange(2), indexing="ij")
    ]
    x = 4 * t[:, None] + 2 * h[:, None] + xp[None]
    angle = (freq(kx)[None] * x % NC) * (2.0 * math.pi / NC)
    sign = np.where(ro == 0, -1.0, 1.0)[:, None]
    inv = np.where(ro[:, None] == ri[None], np.cos(angle), sign * np.sin(angle))
    return split_np(fwd) + split_np(inv)


def phase(sub, pair):
    turn = int(freq(np.array(pair % M))) * sub

    def cosine(k):
        k = k & 7
        half = math.sqrt(0.5)
        near = jnp.where(k == 0, 1.0, jnp.where((k == 1) | (k == 7), half, 0.0))
        return jnp.where(k == 4, -1.0, jnp.where((k == 3) | (k == 5), -half, near)).astype(f32)

    return cosine(turn), cosine(turn + 6)


def split(value):
    hi = value.astype(bf16)
    return hi, (value - hi.astype(f32)).astype(bf16)


def dot(a, b, dims):
    return lax.dot_general(a, b, dims, preferred_element_type=f32)


def dot3(a, b, dims):
    return dot(a[0], b[0], dims) + (dot(a[1], b[0], dims) + dot(a[0], b[1], dims))


def row_iota(shape):
    return lax.broadcasted_iota(jnp.int32, shape, 0)


def lane_iota(shape):
    return lax.broadcasted_iota(jnp.int32, shape, 1)


def swap_rows(value):
    rows = value.shape[0]
    return jnp.where(
        row_iota(value.shape) % 2 == 0, pltpu.roll(value, rows - 1, 0), pltpu.roll(value, 1, 0)
    )


def gelu_parts(v):
    square = v * v
    t = jnp.tanh(SQRT_2_PI * (v + 0.044715 * (square * v)))
    half = 0.5 + 0.5 * t
    return square, t, half


def lift_rows(g, y, heat_ref, cond_ref, lift_ref):
    heat = heat_ref[g, y : y + 1, :]
    cond = cond_ref[g, y : y + 1, :]
    v = lift_ref[0] * heat + lift_ref[1] * cond + lift_ref[2]
    return v * gelu_parts(v)[2]


def store_lifted(heat_ref, cond_ref, lift_ref, hi_ref, lo_ref):
    def group(g, carry):
        rows = pl.ds(pl.multiple_of(g * CH, CH), CH)
        for y in range(16):
            hi, lo = split(lift_rows(g, y, heat_ref, cond_ref, lift_ref))
            hi_ref[rows, y * NC : (y + 1) * NC] = hi
            lo_ref[rows, y * NC : (y + 1) * NC] = lo
        return carry

    lax.fori_loop(0, 8, group, 0, unroll=True)


def send_modes(hi_ref, lo_ref, table_ref, sub, out_ref):
    rows = 2 * DEVICES
    table = jnp.concatenate([table_ref[i] for i in range(8)], axis=1)
    both = dot(table, hi_ref[...], NT)
    modes = both[:rows] + (both[rows:] + dot(table[:rows], lo_ref[...], NT))
    sign = jnp.where(row_iota((8, NC)) % 2 == 0, 1.0, -1.0).astype(f32)
    keep = row_iota((8, NC)) % 4 < 2
    for j in range(64):
        cos, sin = phase(sub, j // 2)
        halves = []
        for h in range(2):
            v = modes[8 * j : 8 * j + 8, h * NC : (h + 1) * NC]
            halves.append(v * cos + swap_rows(v) * (sign * sin))
        first, second = halves
        out_ref[16 * j : 16 * j + 8, :] = jnp.where(keep, first, pltpu.roll(second, 2, 0))
        out_ref[16 * j + 8 : 16 * j + 16, :] = jnp.where(keep, pltpu.roll(first, 6, 0), second)


def pack_kernel(
    heat_hbm, level_hbm, xb_ref, ya_ref, yb_ref, xa_ref, heat_ref, level_ref, sem
):
    copies = [
        pltpu.make_async_copy(heat_hbm, heat_ref, sem.at[0]),
        pltpu.make_async_copy(level_hbm, level_ref, sem.at[1]),
    ]
    for copy in copies:
        copy.start()
    for copy in copies:
        copy.wait()
    at_a = jnp.where(lax.axis_index("tile") % 2 == 0, 4, 0)
    at_b = 4 - at_a
    even = lax.axis_index("sub") % 2 == 0
    for b in range(2):
        for i in range(4):
            for f, source in enumerate((heat_ref, level_ref)):
                xb_ref[f, b, i] = source[b, at_b + i].astype(f32)
                xa_ref[f, b, i] = source[b, at_a + i].astype(f32)
        for i in range(8):
            for f, source in enumerate((heat_ref, level_ref)):
                top = source[b, i, 28:32].astype(f32)
                low = source[b, i, 0:4].astype(f32)
                ya_ref[f, b, i] = jnp.where(even, top, low)
                yb_ref[f, b, i] = jnp.where(even, low, top)


def corner_kernel(ya_ref, yb_ref, xb_ref, corner_b_ref, corner_a_ref):
    at_a = jnp.where(lax.axis_index("tile") % 2 == 0, 4, 0)
    for f in range(2):
        for b in range(2):
            for i in range(4):
                for at, target in ((at_a, corner_a_ref), (4 - at_a, corner_b_ref)):
                    target[f, b, i, 0:4] = ya_ref[f, b, at + i]
                    target[f, b, i, 4:8] = yb_ref[f, b, at + i]


def heat_kernel(
    heat_ref,
    level_ref,
    xa_ref,
    xb_ref,
    ya_ref,
    yb_ref,
    corner_a_ref,
    corner_b_ref,
    lift_ref,
    levels_ref,
    table_ref,
    out_ref,
    hi_ref,
    lo_ref,
    coarse_heat_ref,
    coarse_cond_ref,
    h_ref,
    next_ref,
    c_ref,
    d_ref,
    kx_ref,
    ky_ref,
    kyl_ref,
    kz_ref,
    kzl_ref,
    sum_ref,
    half_ref,
):
    tile = lax.axis_index("tile")
    sub = lax.axis_index("sub")
    even_tile = tile % 2 == 0
    even_sub = sub % 2 == 0
    base_a = jnp.where(even_tile, 12, 0)
    base_b = 12 - base_a
    shape = (40, FN)
    row = row_iota(shape)
    lane = lane_iota(shape)
    last = lane == FN - 1
    first = lane == 0
    top_edge = sub == SUBS - 1
    low_edge = sub == 0
    above = jnp.where(top_edge, 0.0, 1.0).astype(f32)
    below = jnp.where(low_edge, 0.0, 1.0).astype(f32)
    left = jnp.where(tile == 0, 0.0, 1.0).astype(f32)
    right = jnp.where(tile == TILES - 1, 0.0, 1.0).astype(f32)

    def lookup(level):
        bits = [(level & (1 << i)) != 0 for i in range(4)]
        values = [levels_ref[i] for i in range(16)]
        for bit in bits:
            values = [
                jnp.where(bit, values[2 * i + 1], values[2 * i]) for i in range(len(values) // 2)
            ]
        return values[0]

    eight = row_iota((8, FN))
    outer = jnp.where(eight < 4, above, below)

    def outer_layers(i, carry):
        for b in range(2):
            for base, block, corner, side in (
                (base_a, xa_ref, corner_a_ref, jnp.where(even_tile, right, left)),
                (base_b, xb_ref, corner_b_ref, jnp.where(even_tile, left, right)),
            ):
                at = base + i
                h_ref[b, at, 0:32] = block[0, b, i]
                c_ref[b, at, 0:32] = lookup(block[1, b, i].astype(jnp.int32)) * side
                value = corner[0, b, i]
                h_ref[b, at, 32:40] = jnp.where(even_sub, value, pltpu.roll(value, 4, 0))
                value = corner[1, b, i]
                value = jnp.where(even_sub, value, pltpu.roll(value, 4, 0))
                c_ref[b, at, 32:40] = lookup(value.astype(jnp.int32)) * (outer * side)
        return carry

    lax.fori_loop(0, 4, outer_layers, 0, unroll=True)

    def own_layers(i, carry):
        for b in range(2):
            at = 4 + i
            h_ref[b, at, 0:32] = heat_ref[b, i]
            c_ref[b, at, 0:32] = lookup(level_ref[b, i])
            ya = ya_ref[0, b, i]
            yb = yb_ref[0, b, i]
            h_ref[b, at, 32:36] = jnp.where(even_sub, ya, yb)
            h_ref[b, at, 36:40] = jnp.where(even_sub, yb, ya)
            ya = lookup(ya_ref[1, b, i].astype(jnp.int32))
            yb = lookup(yb_ref[1, b, i].astype(jnp.int32))
            c_ref[b, at, 32:36] = jnp.where(even_sub, ya, yb) * above
            c_ref[b, at, 36:40] = jnp.where(even_sub, yb, ya) * below
        return carry

    lax.fori_loop(0, 8, own_layers, 0, unroll=4)

    edge = ((row == 31) & top_edge) | ((row == 39) & low_edge)

    def faces(i, carry):
        for b in range(2):
            c = c_ref[b, i]
            up = pltpu.roll(c, 39, 0)
            down = pltpu.roll(c, 1, 0)
            after = jnp.where(last, 0.0, pltpu.roll(c, FN - 1, 1))
            before = jnp.where(first, 0.0, pltpu.roll(c, 1, 1))
            c_next = c_ref[b, i + 1]
            around = (c_next + c_ref[b, jnp.maximum(i - 1, 0)]) + (up + down) + (after + before)
            d_ref[b, i] = (1.0 - 0.48 * c) - 0.08 * around
            kx_ref[b, i] = 0.08 * (c + c_next)
            ky = jnp.where(edge, 0.0, 0.08 * (c + up))
            ky_ref[b, i] = ky
            kyl_ref[b, i] = pltpu.roll(ky, 1, 0)
            kz_ref[b, i] = jnp.where(last, 0.0, 0.08 * (c + after))
            kzl_ref[b, i] = jnp.where(first, 0.0, 0.08 * (c + before))
        return carry

    lax.fori_loop(0, 15, faces, 0, unroll=5)
    for b in range(2):
        kx_ref[b, 3] = kx_ref[b, 3] * left
        kx_ref[b, 11] = kx_ref[b, 11] * right

    for step in range(1, STEPS + 1):
        source, target = (h_ref, next_ref) if step % 2 == 1 else (next_ref, h_ref)

        def layer_pair(n, carry, source=source, target=target, step=step):
            for j in range(2):
                for b in range(2):
                    i = step + 2 * n + j
                    h = source[b, i]
                    along_x = kx_ref[b, i] * source[b, i + 1] + kx_ref[b, i - 1] * source[b, i - 1]
                    along_y = ky_ref[b, i] * pltpu.roll(h, 39, 0) + kyl_ref[b, i] * pltpu.roll(h, 1, 0)
                    along_z = kz_ref[b, i] * pltpu.roll(h, FN - 1, 1) + kzl_ref[b, i] * pltpu.roll(h, 1, 1)
                    target[b, i] = (d_ref[b, i] * h + along_x) + (along_y + along_z)
            return carry

        lax.fori_loop(0, 8 - step, layer_pair, 0, unroll=True)

    for b in range(2):
        for x in range(4):
            at = 64 * (2 * x + b)
            half_ref[at : at + 32] = h_ref[b, 4 + 2 * x, 0:32] + h_ref[b, 5 + 2 * x, 0:32]
            half_ref[at + 32 : at + 64] = c_ref[b, 4 + 2 * x, 0:32] + c_ref[b, 5 + 2 * x, 0:32]
    pairs = (FN, NC)
    pair = jnp.where(row_iota(pairs) // 2 == lane_iota(pairs), 0.125, 0.0).astype(f32)
    sum_ref[...] = lax.dot_general(
        half_ref[...], pair, NN, precision=highest, preferred_element_type=f32
    )
    for g in range(8):
        for at, target in ((64 * g, coarse_heat_ref), (64 * g + 32, coarse_cond_ref)):
            target[g] = (
                sum_ref[pl.ds(at, 16, stride=2), :] + sum_ref[pl.ds(at + 1, 16, stride=2), :]
            )

    store_lifted(coarse_heat_ref, coarse_cond_ref, lift_ref, hi_ref, lo_ref)
    send_modes(hi_ref, lo_ref, table_ref, sub, out_ref)


def line_modes(in_ref, fwd_hi_ref, fwd_lo_ref):
    sums = []
    for t in range(TILES):
        rows = [in_ref[32 * t + 8 * i : 32 * t + 8 * i + 8, :] for i in range(4)]
        sums.append((rows[0] + rows[1]) + (rows[2] + rows[3]))
    received = split(jnp.concatenate(sums, axis=0))
    both = dot3((fwd_hi_ref[...], fwd_lo_ref[...]), received, NN)
    modes = both[0:32] + pltpu.roll(both[32:64], 64, 1)
    return jnp.concatenate([modes, pltpu.roll(modes, 96, 1)], axis=0)


def mix_kernel(
    in_ref, weight_ref, fwd_hi_ref, fwd_lo_ref, inv_hi_ref, inv_lo_ref, modes_ref, out_ref, w_ref
):
    for kx in range(M):
        for ri in range(2):
            at = kx * 64 + ri * 32
            w_ref[:, at : at + 32] = weight_ref[kx, ri]
    modes = line_modes(in_ref, fwd_hi_ref, fwd_lo_ref)
    modes_ref[...] = modes
    spread = dot3(split(modes[:, 0:32]), split(w_ref[...]), NN)
    shape = (64, NC)
    own = (row_iota(shape) % 32) // 2
    side = lane_iota(shape) // 64
    total = jnp.zeros(shape, f32)
    for part in range(8):
        total = total + jnp.where(own == 2 * part + side, spread[:, part * NC : (part + 1) * NC], 0.0)
    total = total + pltpu.roll(total, 64, 1)
    sign = jnp.where(row_iota(shape) % 2 == 0, -1.0, 1.0).astype(f32)
    mixed = total + sign * swap_rows(pltpu.roll(total, 96, 1))
    mixed = jnp.where(lane_iota(shape) < 32, mixed, 0.0)
    mixed = mixed + pltpu.roll(mixed, 32, 1)
    mixed = mixed + pltpu.roll(mixed, 64, 1)
    mixed = jnp.concatenate([mixed, mixed], axis=0)
    square = (NC, NC)
    mixed = jnp.where(row_iota(square) // 32 == lane_iota(square) // 32, mixed, 0.0)
    lines = dot3((inv_hi_ref[...], inv_lo_ref[...]), split(mixed), NN)
    upper = row_iota((8, NC)) < 4
    for pair in range(16):
        v = lines[8 * pair : 8 * pair + 8]
        turned = pltpu.roll(v, 4, 0)
        for odd, value in enumerate((jnp.where(upper, v, turned), jnp.where(upper, turned, v))):
            for copy in range(4):
                at = (2 * pair + odd) * 32 + 8 * copy
                out_ref[at : at + 8, :] = value


def point_kernel(mix_ref, bias_ref, hi_ref, lo_ref, out_ref, block_ref):
    block_ref[...] = jnp.zeros((BX, BX), f32)
    for g in range(8):
        block_ref[CH * g : CH * g + CH, CH * g : CH * g + CH] = mix_ref[...]
    point = split(jnp.transpose(block_ref[...]))
    bias = jnp.concatenate([bias_ref[...]] * 8, axis=0)
    bias = jnp.concatenate([bias, bias], axis=1)

    def chunk(i, carry):
        cols = pl.ds(pl.multiple_of(i * 256, 256), 256)
        out_ref[:, cols] = dot3(point, (hi_ref[:, cols], lo_ref[:, cols]), NN) + bias
        return carry

    lax.fori_loop(0, 8, chunk, 0)


def field_kernel(
    in_ref,
    base_ref,
    target_ref,
    proj_ref,
    table_hbm,
    prediction_ref,
    out_ref,
    v_ref,
    before_ref,
    hi_ref,
    lo_ref,
    table_ref,
    sem,
):
    copies = [
        pltpu.make_async_copy(table_hbm.at[i], table_ref.at[i], sem.at[i]) for i in range(8)
    ]
    for copy in copies:
        copy.start()
    sub = lax.axis_index("sub")
    sign = jnp.where(row_iota((8, NC)) % 2 == 0, -1.0, 1.0).astype(f32)
    keep = row_iota((8, NC)) % 4 < 2
    for j in range(64):
        cos, sin = phase(sub, j // 2)
        first = in_ref[16 * j : 16 * j + 8, :]
        second = in_ref[16 * j + 8 : 16 * j + 16, :]
        low = jnp.where(keep, first, pltpu.roll(second, 2, 0))
        high = jnp.where(keep, pltpu.roll(first, 6, 0), second)
        for h, v in enumerate((low, high)):
            v_ref[8 * j : 8 * j + 8, h * NC : (h + 1) * NC] = v * cos + swap_rows(v) * (sign * sin)
    modes = split(jnp.transpose(v_ref[...]))
    rows = 2 * DEVICES

    def spectral(i):
        cols = slice(256 * i, 256 * i + 256)
        table = (table_ref[i, :rows], table_ref[i, rows:])
        before_ref[i % 2] = base_ref[:, cols] + dot3(modes, table, NN)

    def pointwise(i):
        for g in range(8):
            x, b = g // 2, g % 2
            group = slice(32 * g, 32 * g + 32)
            for q in range(2):
                y = 2 * i + q
                v = before_ref[i % 2, group, q * NC : (q + 1) * NC]
                square, t, half = gelu_parts(v)
                predicted = jnp.sum(proj_ref[...] * (v * half), axis=0, keepdims=True)
                prediction_ref[b, x, y : y + 1, :] = predicted
                miss = predicted - target_ref[b, x, y : y + 1, :]
                bend = (0.5 * SQRT_2_PI) + (0.5 * SQRT_2_PI * 0.134145) * square
                slope = half + (v * (1.0 - t * t)) * bend
                hi, lo = split(slope * (proj_ref[...] * miss))
                hi_ref[group, y * NC : (y + 1) * NC] = hi
                lo_ref[group, y * NC : (y + 1) * NC] = lo

    copies[0].wait()
    spectral(0)
    for i in range(8):
        if i in (0, 2):
            for copy in copies[1:4] if i == 0 else copies[4:]:
                copy.wait()
        if i < 7:
            spectral(i + 1)
        pointwise(i)
    send_modes(hi_ref, lo_ref, table_ref, sub, out_ref)


def grad_kernel(in_ref, modes_ref, fwd_hi_ref, fwd_lo_ref, out_ref):
    modes_out = line_modes(in_ref, fwd_hi_ref, fwd_lo_ref)
    shape = (64, NC)
    sign = jnp.where(row_iota(shape) % 2 == 0, 1.0, -1.0).astype(f32)
    turned = sign * swap_rows(modes_out)
    right = jnp.where(lane_iota(shape) < 32, modes_out, pltpu.roll(turned, 32, 1))
    left = jnp.transpose(modes_ref[...])[0:32]
    left = jnp.concatenate([left] * M, axis=0) * 0.5
    wide = (32 * M, 64)
    own = row_iota(wide) // 32 == (lane_iota(wide) % 32) // 2
    left = jnp.where(own, left, 0.0)
    grads = dot3(split(left), split(right), NN)
    for kx in range(M):
        block = grads[32 * kx : 32 * kx + 32]
        out_ref[kx, 0] = block[:, 0:32]
        out_ref[kx, 1] = pltpu.roll(block, 96, 1)[:, 0:32]


def vmem():
    return pl.BlockSpec(memory_space=pltpu.VMEM)


def smem():
    return pl.BlockSpec(memory_space=pltpu.SMEM)


def cost(giga):
    return pl.CostEstimate(flops=giga * 10**9, bytes_accessed=2**20, transcendentals=0)


def params(mib):
    return pltpu.CompilerParams(vmem_limit_bytes=int(mib * 1024 * 1024))


def exchange(block):
    return lax.all_to_all(
        block.reshape(DEVICES, 4, NC), ("tile", "sub"), split_axis=0, concat_axis=0, tiled=True
    ).reshape(4 * DEVICES, NC)


def swap(block, axis, odd):
    count = lax.axis_size(axis)
    pairs = []
    for i in range(odd, count - 1, 2):
        pairs += [(i, i + 1), (i + 1, i)]
    return lax.ppermute(block, axis, pairs)


def local(
    initial_heat,
    cond_level,
    cond_table,
    lift_weight,
    lift_bias,
    mix_weight,
    mix_bias,
    proj_weight,
    spectral_weight,
    target_field,
):
    table = jnp.asarray(plane_table())
    fwd_hi, fwd_lo, inv_hi, inv_lo = [jnp.asarray(v) for v in line_tables()]

    with jax.named_scope("halo"):
        sides = jax.ShapeDtypeStruct((2, 2, 4, 32, FN), f32)
        rows = jax.ShapeDtypeStruct((2, 2, 8, 4, FN), f32)
        xb, ya, yb, xa = pl.pallas_call(
            pack_kernel,
            out_shape=(sides, rows, rows, sides),
            in_specs=[pl.BlockSpec(memory_space=pl.ANY)] * 2,
            out_specs=(vmem(),) * 4,
            scratch_shapes=[
                pltpu.VMEM((2, 8, 32, FN), f32),
                pltpu.VMEM((2, 8, 32, FN), jnp.int32),
                pltpu.SemaphoreType.DMA((2,)),
            ],
            compiler_params=params(52.5),
            cost_estimate=cost(8),
        )(initial_heat, cond_level)
        xb = swap(xb, "tile", 1)
        ya = swap(ya, "sub", 0)
        yb = swap(yb, "sub", 1)
        xa = swap(xa, "tile", 0)
        corners = jax.ShapeDtypeStruct((2, 2, 4, 8, FN), f32)
        corner_b, corner_a = pl.pallas_call(
            corner_kernel,
            out_shape=(corners, corners),
            in_specs=[vmem()] * 2 + [pl.BlockSpec(memory_space=pl.ANY)],
            out_specs=(vmem(),) * 2,
            compiler_params=params(8),
            cost_estimate=cost(8),
        )(ya, yb, xb)
        corner_b = swap(corner_b, "tile", 1)
        corner_a = swap(corner_a, "tile", 0)

    lift = jnp.broadcast_to(
        jnp.concatenate([lift_weight, lift_bias[None]], axis=0)[:, :, None], (3, CH, NC)
    )
    bias = jnp.broadcast_to(mix_bias[:, None], (CH, NC))
    proj = jnp.broadcast_to(proj_weight[:, None], (CH, NC))

    lifted = jax.ShapeDtypeStruct((BX, YZ), bf16)
    blocks = jax.ShapeDtypeStruct((4 * DEVICES, NC), f32)
    grid_shape = (2, 16, 40, FN)
    with jax.named_scope("heat"):
        block, lifted_hi, lifted_lo = pl.pallas_call(
            heat_kernel,
            out_shape=(blocks, lifted, lifted),
            in_specs=[vmem()] * 9 + [smem(), vmem()],
            out_specs=(vmem(),) * 3,
            scratch_shapes=[pltpu.VMEM((8, 16, NC), f32)] * 2
            + [pltpu.VMEM(grid_shape, f32)] * 9
            + [
                pltpu.VMEM((512, NC), f32),
                pltpu.VMEM((512, FN), f32),
            ],
            compiler_params=params(24),
            cost_estimate=cost(10),
        )(
            initial_heat,
            cond_level,
            xa,
            xb,
            ya,
            yb,
            corner_a,
            corner_b,
            lift,
            cond_table,
            table,
        )
    block = exchange(block)
    with jax.named_scope("mix"):
        modes_in, block = pl.pallas_call(
            mix_kernel,
            out_shape=(jax.ShapeDtypeStruct((64, NC), f32), blocks),
            in_specs=[vmem()] * 6,
            out_specs=(vmem(),) * 2,
            scratch_shapes=[pltpu.VMEM((CH, 64 * M), f32)],
            compiler_params=params(8),
            cost_estimate=cost(4),
        )(block, spectral_weight.reshape(M, 2, CH, CH), fwd_hi, fwd_lo, inv_hi, inv_lo)
    block = exchange(block)
    with jax.named_scope("point"):
        base = pl.pallas_call(
            point_kernel,
            out_shape=jax.ShapeDtypeStruct((BX, YZ), f32),
            in_specs=[vmem()] * 4,
            out_specs=vmem(),
            scratch_shapes=[pltpu.VMEM((BX, BX), f32)],
            compiler_params=params(8),
            cost_estimate=cost(40),
        )(mix_weight, bias, lifted_hi, lifted_lo)
    with jax.named_scope("field"):
        prediction, block = pl.pallas_call(
            field_kernel,
            out_shape=(jax.ShapeDtypeStruct(target_field.shape, f32), blocks),
            in_specs=[vmem()] * 4 + [pl.BlockSpec(memory_space=pl.ANY)],
            out_specs=(vmem(),) * 2,
            scratch_shapes=[
                pltpu.VMEM((2 * DEVICES, BX), f32),
                pltpu.VMEM((2, BX, 256), f32),
                pltpu.VMEM((BX, YZ), bf16),
                pltpu.VMEM((BX, YZ), bf16),
                pltpu.VMEM((8, 4 * DEVICES, 256), bf16),
                pltpu.SemaphoreType.DMA((8,)),
            ],
            compiler_params=params(50),
            cost_estimate=cost(6),
        )(block, base, target_field, proj, table)
    block = exchange(block)
    with jax.named_scope("grad"):
        spectral_grad = pl.pallas_call(
            grad_kernel,
            out_shape=jax.ShapeDtypeStruct((M, 2, CH, CH), f32),
            in_specs=[vmem()] * 4,
            out_specs=vmem(),
            compiler_params=params(8),
        )(block, modes_in, fwd_hi, fwd_lo)
    return (prediction, spectral_grad.reshape(1, 1, M, 2, CH, CH))


def solution(mesh):
    in_specs = (
        P(None, "tile", "sub", None),
        P(None, "tile", "sub", None),
        P(),
        P(),
        P(),
        P(),
        P(),
        P(),
        P("sub", "tile", None, None, None, None),
        P(None, "tile", "sub", None),
    )
    out_specs = (P(None, "tile", "sub", None), P("sub", "tile", None, None, None, None))
    return jax.shard_map(local, mesh=mesh, in_specs=in_specs, out_specs=out_specs, check_vma=False)
```
